512 devices in a mesh: dp: 32 (over z, core), tensor: 16 (over x, y).
Axes of the slice: x: 4, y: 4, z: 16, core: 2. Of those that a mesh axis runs over, the one named last changes fastest.
Arguments:
- activations: bfloat16 [65536, 4096], P(('dp', 'tensor')), may hold values from -6 to 6
- grad_query: bfloat16 [65536, 4096], P('dp', 'tensor'), may hold values from -6 to 6
- feedback: bfloat16 [131072, 4096], P('dp', 'tensor'), may hold values from -256 to 256
- start_factor: float32 [8, 4096], P(None, 'tensor'), may hold values from -6 to 6
Outputs:
- basis: float32 [128, 4096], P('tensor')
- coeffs: float32 [8, 4096], P(None, 'tensor')
The draws below stay inside these ranges and needn't reach their ends.
All inputs are finite; a program needn't handle non-finite values.
Results may differ from the reference program's by a relative error of at most 0.0003.
Values may be sent and summed in bfloat16 or wider, within the bound.
A program may use at most 64 MiB of HBM per device.

```python
import jax
import jax.numpy as jnp
from jax import lax

D = 4096
HEADS_DEV = 2
HEAD = 128
RANK = 8
TOK = 2048
ROWS = 65536
COLS = 4096
FEED_ROWS = 131072
N_DP = 32
N_TENSOR = 16


def block_levels(key, shape, cuts, smallest, top_value):
    level, own = 1.0, jax.random.fold_in(key, 6)
    for dim, shards_of in cuts:
        draws = jnp.exp(jax.random.uniform(jax.random.fold_in(own, dim), (shards_of,), jnp.float32, smallest / len(cuts), top_value / len(cuts)))
        level = level * jnp.repeat(draws, shape[dim] // shards_of).reshape([-1 if axis == dim else 1 for axis in range(len(shape))])
    return level


def bell_draw(stream_key, shape, scale, most, pieces=(), kind=jnp.bfloat16):
    drawn = jax.random.normal(stream_key, shape, jnp.float32) * scale
    if len(pieces) > 0:
        drawn = block_levels(stream_key, shape, pieces, -0.22, 0.18) * drawn
    return jnp.clip(drawn, min=-most, max=most).astype(kind)


def setup_inputs(seed: int = 0) -> dict:
    seeds = jax.random.split(jax.random.key(seed), 5)
    activations = bell_draw(seeds[0], (ROWS, D), 1.0, 6.0, ((0, 512),))
    grad_query = bell_draw(seeds[1], (ROWS, COLS), 1.0, 6.0, ((0, 32), (1, 16)))
    feedback = bell_draw(seeds[2], (FEED_ROWS, COLS), (TOK ** 0.5), 256.0, ((0, 32), (1, 16)))
    start_factor = bell_draw(seeds[3], (RANK, COLS), 1.0, 6.0, ((1, 16),), jnp.float32)
    return {"activations": activations, "grad_query": grad_query, "feedback": feedback, "start_factor": start_factor}


EPSILON = 1e-06
HIGHEST = lax.Precision.HIGHEST

def orthonormal_rows(factor):
    finished = []
    for position in range(factor.shape[0]):
        vector = factor[position]
        for earlier in finished:
            vector = vector - jnp.sum(earlier * vector) * earlier
        vector = vector / jnp.sqrt(jnp.sum(vector * vector) + EPSILON)
        finished.append(vector)
    return jnp.stack(finished)

def reference(activations, grad_query, feedback, start_factor):
    width = HEADS_DEV * HEAD
    acts_all = activations.reshape(N_DP, TOK, D)
    grads_all = grad_query.reshape(N_DP, TOK, N_TENSOR, width)
    errors_all = feedback.reshape(N_DP, D, N_TENSOR, width)
    starting = start_factor.astype(jnp.float32).reshape(RANK, N_TENSOR, width)

    def corrected(tokens, grads, errors):
        grad_weight = jnp.einsum('sd,snh->dnh', tokens.astype(jnp.float32), grads.astype(jnp.float32), precision=HIGHEST)
        return grad_weight + errors.astype(jnp.float32)

    def first_pass(total, inputs):
        tokens, grads, errors = inputs
        whole = corrected(tokens, grads, errors)
        return (total + jnp.einsum('rnh,dnh->nrd', starting, whole, precision=HIGHEST), 0)
    left, unused = lax.scan(first_pass, jnp.zeros((N_TENSOR, RANK, D), jnp.float32), (acts_all, grads_all, errors_all))
    basis = jax.vmap(orthonormal_rows)(left)

    def second_pass(total, inputs):
        tokens, grads, errors = inputs
        whole = corrected(tokens, grads, errors)
        return (total + jnp.einsum('nrd,dnh->nrh', basis, whole, precision=HIGHEST), 0)
    right, unused_two = lax.scan(second_pass, jnp.zeros((N_TENSOR, RANK, width), jnp.float32), (acts_all, grads_all, errors_all))
    coeffs = jnp.transpose(right / N_DP, (1, 0, 2)).reshape(RANK, N_TENSOR * width)
    return (basis.reshape(N_TENSOR * RANK, D), coeffs)
```

```python
import functools

import jax
import jax.numpy as jnp
from jax import lax
from jax.experimental import pallas as pl
from jax.experimental.pallas import tpu as pltpu
from jax.sharding import PartitionSpec as P

EPSILON = 1e-06
MESH = pl.DeviceIdType.MESH
F32, BF16 = jnp.float32, jnp.bfloat16
RANK = 8
LANES = 128
NT = (((1,), (1,)), ((), ()))
NN = (((1,), (0,)), ((), ()))


def dot(a, b, dims):
    return lax.dot_general(a, b, dims, preferred_element_type=F32)


def pair(value):
    top = value.astype(BF16).astype(F32)
    return jnp.concatenate([top, value - top], axis=0).astype(BF16)


def unpair(value):
    return value[:RANK] + value[RANK:]


def wait_bytes(ref, sem):
    pltpu.make_async_copy(ref, ref, sem).wait()


def kernel(
    nx, ny, nz,
    s_ref, g_hbm, a_hbm, f_hbm,
    basis_ref, coeffs_ref,
    g_v, a_v, f_v, gh_v, fh_v,
    psend, precv,
    la, lb, ra, rb, sa, sb, r2a, r2b,
    lf, lfr, zs, zr, full,
    bp, ball_a, ball_b,
    qs, qr, cr, cfin,
    local, send, recv,
):
    tn = nx * ny
    half = a_v.shape[1]
    quarter = half // 2
    tok = g_v.shape[0]
    dp, t = lax.axis_index("dp"), lax.axis_index("tensor")
    z, c = dp // 2, lax.rem(dp, 2)
    o = 1 - c
    x, y = t // ny, lax.rem(t, ny)
    partner = (2 * z + o, t)

    def cols(index, size):
        return pl.ds(pl.multiple_of(index * size, size), size)

    def rows(index, size):
        return pl.ds(pl.multiple_of(index * size, size), size)

    def remote(src, dst, index, device):
        return pltpu.make_async_remote_copy(
            src_ref=src, dst_ref=dst, send_sem=send.at[index], recv_sem=recv.at[index],
            device_id=device, device_id_type=MESH,
        )

    def plane(k):
        other = lax.rem(t + k // 2, tn)
        return other, (2 * z + lax.rem(c + lax.rem(k, 2), 2), other)

    def along_z(k):
        other = lax.rem(z + k, nz)
        return other, (2 * other + c, t)

    def along_x(k):
        other = lax.rem(x + k, nx)
        return other, (dp, other * ny + y)

    def along_y(k):
        other = lax.rem(y + k, ny)
        return other, (dp, x * ny + other)

    loads = [
        pltpu.make_async_copy(g_hbm, g_v, local.at[0]),
        pltpu.make_async_copy(a_hbm.at[:, cols(c, half)], a_v.at[rows(c, LANES), :], local.at[1]),
        pltpu.make_async_copy(f_hbm, f_v, local.at[2]),
        pltpu.make_async_copy(g_hbm.at[:, cols(c, LANES)], gh_v.at[c], local.at[3]),
        pltpu.make_async_copy(f_hbm.at[:, cols(c, LANES)], fh_v.at[c], local.at[4]),
    ]
    for load in loads:
        load.start()

    barrier = pltpu.get_barrier_semaphore()

    @pl.loop(1, 2 * tn)
    def _(k):
        pl.semaphore_signal(barrier, inc=1, device_id=plane(k)[1], device_id_type=MESH)

    @pl.loop(1, nz)
    def _(k):
        pl.semaphore_signal(barrier, inc=1, device_id=along_z(k)[1], device_id_type=MESH)

    s2 = pair(s_ref[...])
    loads[0].wait()
    p2 = pair(unpair(dot(s2, g_v[...], NT)))
    for k in range(tn):
        psend[k] = p2[:, k * LANES:(k + 1) * LANES]

    pl.semaphore_wait(barrier, 2 * tn - 1 + nz - 1)

    share_a = remote(a_hbm.at[:, cols(o, half)], a_v.at[rows(c, LANES), :], 0, partner)
    share_a.start()

    precv[rows(c * tn + t, 16), :] = psend[t]

    @pl.loop(1, 2 * tn)
    def _(k):
        other, device = plane(k)
        remote(psend.at[other], precv.at[rows(c * tn + t, 16), :], 1, device).start()

    share_g = remote(g_hbm.at[:, cols(o, LANES)], gh_v.at[c], 2, partner)
    share_g.start()
    share_f = remote(f_hbm.at[:, cols(o, LANES)], fh_v.at[c], 3, partner)
    share_f.start()

    loads[1].wait()
    share_a.wait()
    p_all = precv.at[pl.ds(0, (2 * tn - 1) * 16), :]
    wait_bytes(p_all, recv.at[1])

    lhs = jnp.concatenate([precv[:tn * 16, :], precv[tn * 16:, :]], axis=1)
    step = min(512, quarter)
    for j in range(quarter // step):
        at = slice(j * step, (j + 1) * step)
        part = dot(lhs, a_v[:, at], NN)
        for gx in range(nx):
            for gy in range(ny):
                g = gx * ny + gy
                la[gx, gy, :, at] = unpair(part[g * 16:(g + 1) * 16])
    for k in range(1, nx):
        other, device = along_x(k)
        remote(la.at[other], ra.at[x], 4, device).start()
    for j in range(quarter // step):
        at = slice(j * step, (j + 1) * step)
        part = dot(lhs, a_v[:, quarter + j * step:quarter + (j + 1) * step], NN)
        for gx in range(nx):
            for gy in range(ny):
                g = gx * ny + gy
                lb[gy, gx, :, at] = unpair(part[g * 16:(g + 1) * 16])
    for k in range(1, ny):
        other, device = along_y(k)
        remote(lb.at[other], rb.at[y], 5, device).start()

    loads[2].wait()
    for h in range(2):
        lf[h] = unpair(dot(s2, f_v[h * half:(h + 1) * half, :], NT))
    share_l = remote(lf.at[o], lfr, 6, partner)
    share_l.start()

    wait_bytes(ra.at[pl.ds(0, nx - 1)], recv.at[4])
    total = la[x]
    for k in range(1, nx):
        total = total + ra[lax.rem(x + k, nx)]
    sa[...] = total
    for k in range(1, ny):
        other, device = along_y(k)
        remote(sa.at[other], r2a.at[y], 7, device).start()
    wait_bytes(rb.at[pl.ds(0, ny - 1)], recv.at[5])
    total = lb[y]
    for k in range(1, ny):
        total = total + rb[lax.rem(y + k, ny)]
    sb[...] = total
    for k in range(1, nx):
        other, device = along_x(k)
        remote(sb.at[other], r2b.at[x], 8, device).start()

    share_l.wait()
    feed = lf[c] + lfr[...]
    wait_bytes(r2a.at[pl.ds(0, ny - 1)], recv.at[7])
    total = sa[y] + feed[:, :quarter]
    for k in range(1, ny):
        total = total + r2a[lax.rem(y + k, ny)]
    for k in range(nz // 2):
        zs[k] = total[:, k * LANES:(k + 1) * LANES]
    wait_bytes(r2b.at[pl.ds(0, nx - 1)], recv.at[8])
    total = sb[x] + feed[:, quarter:]
    for k in range(1, nx):
        total = total + r2b[lax.rem(x + k, nx)]
    for k in range(nz // 2):
        zs[nz // 2 + k] = total[:, k * LANES:(k + 1) * LANES]

    zr[z] = zs[z]

    @pl.loop(1, nz)
    def _(k):
        other, device = along_z(k)
        remote(zs.at[other], zr.at[z], 9, device).start()

    wait_bytes(zr.at[pl.ds(0, nz - 1)], recv.at[9])
    total = zr[0]
    for k in range(1, nz):
        total = total + zr[k]
    full[c, z] = total

    @pl.loop(1, nz)
    def _(k):
        other, device = along_z(k)
        remote(full.at[c, z], full.at[c, z], 10, device).start()

    wait_bytes(full.at[c, pl.ds(0, nz - 1)], recv.at[10])
    share_full = remote(full.at[c], full.at[c], 11, partner)
    share_full.start()
    share_full.wait()

    v = [full[h, k] for h in range(2) for k in range(nz)]
    row = lax.broadcasted_iota(jnp.int32, (RANK, 1), 0)
    scale = jnp.zeros((RANK, 1), F32)
    for i in range(RANK):
        own = [jnp.broadcast_to(u[i:i + 1, :], u.shape) for u in v]
        prods = [a * b for a, b in zip(own, v)]
        while len(prods) > 1:
            prods = [a + b for a, b in zip(prods[::2], prods[1::2])]
        dots = jnp.sum(prods[0], axis=1, keepdims=True)
        square = dots[i:i + 1, :] + EPSILON
        scale = jnp.where(row == i, 1.0 / jnp.sqrt(square), scale)
        factor = jnp.where(row > i, dots / square, 0.0)
        v = [u - factor * a for u, a in zip(v, own)]
    for h in range(2):
        for k in range(nz):
            unit = v[h * nz + k] * scale
            basis_ref[:, (h * nz + k) * LANES:(h * nz + k + 1) * LANES] = unit
            bp[h, :, k * LANES:(k + 1) * LANES] = pair(unit)

    ball_a[x, y] = bp[c, :, :quarter]
    ball_b[x, y] = bp[c, :, quarter:]
    for k in range(1, nx):
        other, device = along_x(k)
        remote(ball_a.at[x, y], ball_a.at[x, y], 12, device).start()
    for k in range(1, ny):
        other, device = along_y(k)
        remote(ball_b.at[x, y], ball_b.at[x, y], 13, device).start()
    wait_bytes(ball_a.at[0, pl.ds(0, nx - 1)], recv.at[12])
    for k in range(1, ny):
        other, device = along_y(k)
        remote(ball_a.at[:, y], ball_a.at[:, y], 14, device).start()
    wait_bytes(ball_b.at[0, pl.ds(0, ny - 1)], recv.at[13])
    for k in range(1, nx):
        other, device = along_x(k)
        remote(ball_b.at[x], ball_b.at[x], 15, device).start()

    loads[4].wait()
    share_f.wait()
    right = dot(bp[0], fh_v[0, :half, :], NN) + dot(bp[1], fh_v[0, half:, :], NN)
    right = right + dot(bp[0], fh_v[1, :half, :], NN) + dot(bp[1], fh_v[1, half:, :], NN)

    wait_bytes(ball_a.at[:, pl.ds(0, ny - 1)], recv.at[14])
    q2 = dot(ball_a[...].reshape(tn * 16, quarter), a_v[:, :quarter], NT)
    wait_bytes(ball_b.at[pl.ds(0, nx - 1)], recv.at[15])
    q2 = q2 + dot(ball_b[...].reshape(tn * 16, quarter), a_v[:, quarter:], NT)
    for g in range(tn):
        qs[g] = unpair(q2[g * 16:(g + 1) * 16])

    qr[c * tn + t] = qs[t]

    @pl.loop(1, 2 * tn)
    def _(k):
        other, device = plane(k)
        remote(qs.at[other], qr.at[c * tn + t], 16, device).start()

    loads[3].wait()
    share_g.wait()
    wait_bytes(qr.at[pl.ds(0, 2 * tn - 1)], recv.at[16])
    parts = [pair(qr[k] + qr[tn + k]) for k in range(tn)]
    for h in range(2):
        q = jnp.concatenate([u[:, h * LANES:(h + 1) * LANES] for u in parts], axis=1)
        right = right + dot(q, gh_v[h], NN)
    cr[z] = unpair(right)

    @pl.loop(1, nz)
    def _(k):
        other, device = along_z(k)
        remote(cr.at[z], cr.at[z], 17, device).start()

    wait_bytes(cr.at[pl.ds(0, nz - 1)], recv.at[17])
    total = cr[0]
    for k in range(1, nz):
        total = total + cr[k]
    total = total * (1.0 / (2 * nz))
    cfin[...] = total
    coeffs_ref[:, cols(c, LANES)] = total
    share_c = remote(cfin, coeffs_ref.at[:, cols(c, LANES)], 18, partner)
    share_c.start()
    share_c.wait()

    wait_bytes(p_all, send.at[1])
    wait_bytes(ra.at[pl.ds(0, nx - 1)], send.at[4])
    wait_bytes(rb.at[pl.ds(0, ny - 1)], send.at[5])
    wait_bytes(r2a.at[pl.ds(0, ny - 1)], send.at[7])
    wait_bytes(r2b.at[pl.ds(0, nx - 1)], send.at[8])
    wait_bytes(zr.at[pl.ds(0, nz - 1)], send.at[9])
    wait_bytes(full.at[c, pl.ds(0, nz - 1)], send.at[10])
    wait_bytes(ball_a.at[0, pl.ds(0, nx - 1)], send.at[12])
    wait_bytes(ball_b.at[0, pl.ds(0, ny - 1)], send.at[13])
    wait_bytes(ball_a.at[:, pl.ds(0, ny - 1)], send.at[14])
    wait_bytes(ball_b.at[pl.ds(0, nx - 1)], send.at[15])
    wait_bytes(qr.at[pl.ds(0, 2 * tn - 1)], send.at[16])
    wait_bytes(cr.at[pl.ds(0, nz - 1)], send.at[17])


def body(nx, ny, activations, grad_query, feedback, start_factor):
    tn = nx * ny
    nz = lax.axis_size("dp") // 2
    d = activations.shape[1]
    half, quarter = d // 2, d // 4
    tok, width = grad_query.shape
    vm = pltpu.VMEM
    scratch = [
        vm((tok, width), BF16),
        vm((2 * LANES, half), BF16),
        vm((d, width), BF16),
        vm((2, tok, LANES), BF16),
        vm((2, d, LANES), BF16),
        vm((tn, 16, LANES), BF16),
        vm((2 * tn * 16, LANES), BF16),
        vm((nx, ny, RANK, quarter), F32),
        vm((ny, nx, RANK, quarter), F32),
        vm((nx, ny, RANK, quarter), F32),
        vm((ny, nx, RANK, quarter), F32),
        vm((ny, RANK, quarter), F32),
        vm((nx, RANK, quarter), F32),
        vm((ny, RANK, quarter), F32),
        vm((nx, RANK, quarter), F32),
        vm((2, RANK, half), F32),
        vm((RANK, half), F32),
        vm((nz, RANK, LANES), F32),
        vm((nz, RANK, LANES), F32),
        vm((2, nz, RANK, LANES), F32),
        vm((2, 16, half), BF16),
        vm((nx, ny, 16, quarter), BF16),
        vm((nx, ny, 16, quarter), BF16),
        vm((tn, RANK, 2 * LANES), F32),
        vm((2 * tn, RANK, 2 * LANES), F32),
        vm((nz, RANK, LANES), F32),
        vm((RANK, LANES), F32),
        pltpu.SemaphoreType.DMA((5,)),
        pltpu.SemaphoreType.DMA((19,)),
        pltpu.SemaphoreType.DMA((19,)),
    ]
    anywhere = pl.BlockSpec(memory_space=pl.ANY)
    inside = pl.BlockSpec(memory_space=pltpu.VMEM)
    return pl.pallas_call(
        functools.partial(kernel, nx, ny, nz),
        out_shape=(
            jax.ShapeDtypeStruct((RANK, d), F32),
            jax.ShapeDtypeStruct((RANK, width), F32),
        ),
        in_specs=[inside, anywhere, anywhere, anywhere],
        out_specs=(inside, inside),
        scratch_shapes=scratch,
        compiler_params=pltpu.CompilerParams(
            collective_id=0, has_side_effects=True, vmem_limit_bytes=48 * 1024 * 1024
        ),
    )(start_factor, grad_query, activations, feedback)


def solution(mesh):
    side = 4 if mesh.shape["tensor"] == 16 else 2
    in_specs = (P(("dp", "tensor"), None), P("dp", "tensor"), P("dp", "tensor"), P(None, "tensor"))
    out_specs = (P("tensor", None), P(None, "tensor"))
    return jax.shard_map(
        functools.partial(body, side, mesh.shape["tensor"] // side),
        mesh=mesh, in_specs=in_specs, out_specs=out_specs, check_vma=False,
    )
```

```python
import functools
import itertools

import jax
import jax.numpy as jnp
from jax import lax
from jax.experimental import pallas as pl
from jax.experimental.pallas import tpu as pltpu
from jax.sharding import PartitionSpec as P

EPSILON = 1e-06
MESH = pl.DeviceIdType.MESH
F32, BF16 = jnp.float32, jnp.bfloat16
RANK = 8
LANES = 128
NT = (((1,), (1,)), ((), ()))
NN = (((1,), (0,)), ((), ()))
NEAR_A, FAR_A, FAR_B, NEAR_B = range(4)
CHANNELS = 48


def dot(a, b, dims):
    return lax.dot_general(a, b, dims, preferred_element_type=F32)


def pair(value):
    top = value.astype(BF16).astype(F32)
    return jnp.concatenate([top, value - top], axis=0).astype(BF16)


def unpair(value):
    return value[:RANK] + value[RANK:]


def wait_bytes(ref, sem):
    pltpu.make_async_copy(ref, ref, sem).wait()


def hops(k, n):
    return min(k, n - k)


def kernel(
    nx, ny, nz,
    s_hbm, g_hbm, a_hbm, f_hbm,
    basis_hbm, coeffs_ref,
    s_v, g_v, a_v, f_v, gh_v, fh_v,
    psend, precv,
    first, first_in, second, second_in,
    lf, lfr, zs, zr,
    ball, other_half, basis_v, qacc,
    qs, qr, cr, cfin,
    local, send, recv, ready,
):
    tn = nx * ny
    half = a_v.shape[1]
    slots = nz // 4
    dp, t = lax.axis_index("dp"), lax.axis_index("tensor")
    z, c = dp // 2, lax.rem(dp, 2)
    o = 1 - c
    x, y = t // ny, lax.rem(t, ny)
    partner = (2 * z + o, t)
    xs = [x] + [lax.rem(x + k, nx) for k in range(1, nx)]
    ys = [y] + [lax.rem(y + k, ny) for k in range(1, ny)]
    around = [z] + [lax.rem(z + k, nz) for k in range(1, nz)]

    def block(index, size):
        return pl.ds(pl.multiple_of(index * size, size), size)

    counter = itertools.count()
    sent = []

    def remote(src, dst, channel, device):
        return pltpu.make_async_remote_copy(
            src_ref=src, dst_ref=dst, send_sem=send.at[channel], recv_sem=recv.at[channel],
            device_id=device, device_id_type=MESH,
        )

    def arrived(ref, channel):
        wait_bytes(ref, recv.at[channel])
        sent.append((ref, channel))

    def along_z(k):
        return (2 * around[k] + c, t)

    def along_x(k):
        return (dp, xs[k] * ny + y)

    def along_y(k):
        return (dp, x * ny + ys[k])

    plane = []
    for dx, dy, dc in itertools.product(range(nx), range(ny), range(2)):
        if dx + dy + dc:
            group = xs[dx] * ny + ys[dy]
            plane.append((hops(dx, nx) + hops(dy, ny), group, (2 * z + o if dc else dp, group)))
    plane.sort(key=lambda entry: -entry[0])
    by_distance = sorted(range(1, nz), key=lambda k: -hops(k, nz))

    load_s = pltpu.make_async_copy(s_hbm, s_v, local.at[0])
    load_g = pltpu.make_async_copy(g_hbm, g_v, local.at[1])
    load_a = pltpu.make_async_copy(a_hbm.at[:, block(c, half)], a_v.at[block(c, LANES), :], local.at[2])
    load_f = pltpu.make_async_copy(f_hbm, f_v, local.at[3])
    load_gh = pltpu.make_async_copy(g_hbm.at[:, block(c, LANES)], gh_v.at[c], local.at[4])
    load_fh = pltpu.make_async_copy(f_hbm.at[:, block(c, LANES)], fh_v.at[c], local.at[5])
    load_s.start()
    load_g.start()

    barrier = pltpu.get_barrier_semaphore()
    beside = sorted({1, nz - 1})
    for _, _, device in plane:
        pl.semaphore_signal(barrier, inc=1, device_id=device, device_id_type=MESH)
    for k in beside:
        pl.semaphore_signal(barrier, inc=1, device_id=along_z(k), device_id_type=MESH)
    for load in (load_a, load_f, load_gh, load_fh):
        load.start()

    reach = [2 ** k for k in range(8) if 2 ** k < nz // 2]

    def tell(step):
        for k in (reach[step], nz - reach[step]):
            pl.semaphore_signal(ready.at[step], inc=1, device_id=along_z(k), device_id_type=MESH)

    load_s.wait()
    s2 = pair(s_v[...])
    load_g.wait()
    p2 = pair(unpair(dot(s2, g_v[...], NT)))
    for k in range(tn):
        psend[k] = p2[:, k * LANES:(k + 1) * LANES]

    pl.semaphore_wait(barrier, len(plane) + len(beside))

    p_channel = next(counter)
    for _, group, device in plane:
        remote(psend.at[group], precv.at[block(c * tn + t, 16), :], p_channel, device).start()
    share_a = remote(a_hbm.at[:, block(o, half)], a_v.at[block(c, LANES), :], next(counter), partner)
    share_a.start()
    tell(0)
    precv[block(c * tn + t, 16), :] = psend[t]
    share_g = remote(g_hbm.at[:, block(o, LANES)], gh_v.at[c], next(counter), partner)
    share_g.start()
    share_f = remote(f_hbm.at[:, block(o, LANES)], fh_v.at[c], next(counter), partner)
    share_f.start()

    load_a.wait()
    share_a.wait()
    arrived(precv.at[pl.ds(0, (2 * tn - 1) * 16), :], p_channel)

    def features(k):
        return a_v[:, block(around[k], LANES)]

    def region(r):
        return range(r * slots, (r + 1) * slots)

    def order(r):
        on_x, on_y = (x, nx, xs, along_x), (y, ny, ys, along_y)
        return (on_x, on_y) if r in (NEAR_A, FAR_A) else (on_y, on_x)

    lhs = jnp.concatenate([precv[:tn * 16, :], precv[tn * 16:, :]], axis=1)
    first_channel, second_channel = {}, {}
    for r in (FAR_A, FAR_B, NEAR_A, NEAR_B):
        (here, count, _, device), _ = order(r)
        part = dot(lhs, jnp.concatenate([features(k) for k in region(r)], axis=1), NN)
        for gx in range(nx):
            for gy in range(ny):
                g = gx * ny + gy
                i, j = (gx, gy) if r in (NEAR_A, FAR_A) else (gy, gx)
                first[r, i, j] = unpair(part[g * 16:(g + 1) * 16])
        first_channel[r] = next(counter)
        others = order(r)[0][2]
        for k in range(1, count):
            remote(first.at[r, others[k]], first_in.at[r, here], first_channel[r], device(k)).start()
    if len(reach) > 1:
        pl.semaphore_wait(ready.at[0], 2)
        tell(1)

    load_f.wait()
    for h in range(2):
        for k in range(nz):
            at = (h * nz + k) * LANES
            lf[h, k] = unpair(dot(s2, f_v[at:at + LANES, :], NT))
    share_l = remote(lf.at[o], lfr, next(counter), partner)
    share_l.start()

    for r in (FAR_A, FAR_B, NEAR_A, NEAR_B):
        (here, count, others, _), (place, size, beyond, device) = order(r)
        arrived(first_in.at[r, pl.ds(0, count - 1)], first_channel[r])
        total = first[r, here]
        for k in range(1, count):
            total = total + first_in[r, others[k]]
        second[r] = total
        second_channel[r] = next(counter)
        for k in range(1, size):
            remote(second.at[r, beyond[k]], second_in.at[r, place], second_channel[r], device(k)).start()
    if len(reach) > 2:
        pl.semaphore_wait(ready.at[1], 2)
        tell(2)

    share_l.wait()
    z_channel = next(counter)
    for r in (FAR_A, FAR_B, NEAR_A, NEAR_B):
        _, (place, size, beyond, _) = order(r)
        arrived(second_in.at[r, pl.ds(0, size - 1)], second_channel[r])
        total = second[r, place]
        for k in range(1, size):
            total = total + second_in[r, beyond[k]]
        for i, k in enumerate(region(r)):
            zs[k] = total[:, i * LANES:(i + 1) * LANES] + (lf[c, around[k]] + lfr[around[k]])
        if r == FAR_A:
            for step in range(max(len(reach) - 1, 0), len(reach)):
                pl.semaphore_wait(ready.at[step], 2)
        for k in sorted(region(r), key=lambda k: -hops(k, nz)):
            if k:
                remote(zs.at[k], zr.at[k], z_channel, along_z(k)).start()
    arrived(zr.at[pl.ds(0, nz - 1)], z_channel)
    total = zs[0]
    for k in range(1, nz):
        total = total + zr[k]

    ball[x, y, 0] = pair(total)
    gather = [next(counter) for _ in range(4)]
    for k in by_distance:
        remote(ball.at[x, y, 0], ball.at[x, y, k], gather[k // slots], along_z(nz - k)).start()

    def part_of(r):
        return pl.ds(r * slots, slots)

    def spread_own(r):
        own = part_of(r)
        if r == NEAR_A:
            if slots > 1:
                arrived(ball.at[x, y, pl.ds(0, slots - 1)], gather[r])
        else:
            arrived(ball.at[x, y, own], gather[r])
        first_channel[r] = next(counter)
        (_, count, _, device), _ = order(r)
        for k in range(1, count):
            remote(ball.at[x, y, own], ball.at[x, y, own], first_channel[r], device(k)).start()

    def spread_line(r):
        own = part_of(r)
        (_, count, _, _), (_, size, _, device) = order(r)
        arrived(ball.at[x, pl.ds(0, count - 1), own], first_channel[r])
        second_channel[r] = next(counter)
        line = ball.at[:, y, own] if r in (NEAR_A, FAR_A) else ball.at[x, :, own]
        for k in range(1, size):
            remote(line, line, second_channel[r], device(k)).start()

    def product(r):
        own = part_of(r)
        _, (_, size, _, _) = order(r)
        rest = ball.at[:, pl.ds(0, size - 1), own] if r in (NEAR_A, FAR_A) else ball.at[pl.ds(0, size - 1), :, own]
        arrived(rest, second_channel[r])
        left = jnp.concatenate([ball[:, :, k].reshape(tn * 16, LANES) for k in region(r)], axis=1)
        return dot(left, jnp.concatenate([features(k) for k in region(r)], axis=1), NT)

    spread_own(NEAR_A)
    spread_own(NEAR_B)
    spread_line(NEAR_A)
    spread_line(NEAR_B)
    spread_own(FAR_A)
    spread_own(FAR_B)
    share_half = remote(ball.at[x, y], other_half, next(counter), partner)
    share_half.start()
    qacc[...] = product(NEAR_A) + product(NEAR_B)
    spread_line(FAR_A)
    spread_line(FAR_B)

    share_half.wait()
    pairs = []
    for h in range(2):
        for k in range(nz):
            slot = lax.rem(k - z + nz, nz)
            pairs.append(jnp.where(c == h, ball[x, y, slot].astype(F32), other_half[slot].astype(F32)))
    v = [unpair(u) for u in pairs]
    row = lax.broadcasted_iota(jnp.int32, (RANK, 1), 0)
    ops = (lax.broadcasted_iota(jnp.int32, (RANK, LANES), 0) == lax.broadcasted_iota(jnp.int32, (RANK, LANES), 1)).astype(F32)
    scale = jnp.zeros((RANK, 1), F32)
    for i in range(RANK):
        own = [jnp.broadcast_to(u[i:i + 1, :], u.shape) for u in v]
        prods = [a * b for a, b in zip(own, v)]
        while len(prods) > 1:
            prods = [a + b for a, b in zip(prods[::2], prods[1::2])]
        dots = jnp.sum(prods[0], axis=1, keepdims=True)
        square = dots[i:i + 1, :] + EPSILON
        scale = jnp.where(row == i, 1.0 / jnp.sqrt(square), scale)
        factor = jnp.where(row > i, dots / square, 0.0)
        v = [u - factor * a for u, a in zip(v, own)]
        ops = ops - factor * jnp.broadcast_to(ops[i:i + 1, :], ops.shape)
    ops = ops * scale
    for k, u in enumerate(v):
        basis_v[:, k * LANES:(k + 1) * LANES] = u * scale
    store_basis = pltpu.make_async_copy(basis_v, basis_hbm, local.at[6])
    store_basis.start()

    load_fh.wait()
    share_f.wait()
    left = jnp.concatenate([u.astype(BF16) for u in pairs], axis=1)
    right = dot(left, fh_v[0], NN) + dot(left, fh_v[1], NN)

    q2 = qacc[...] + product(FAR_A) + product(FAR_B)
    for g in range(tn):
        qs[g] = unpair(q2[g * 16:(g + 1) * 16])
    q_channel = next(counter)
    for _, group, device in plane:
        remote(qs.at[group], qr.at[c * tn + t], q_channel, device).start()
    qr[c * tn + t] = qs[t]

    load_gh.wait()
    share_g.wait()
    arrived(qr.at[pl.ds(0, 2 * tn - 1)], q_channel)
    parts = [pair(qr[k] + qr[tn + k]) for k in range(tn)]
    for h in range(2):
        q = jnp.concatenate([u[:, h * LANES:(h + 1) * LANES] for u in parts], axis=1)
        right = right + dot(q, gh_v[h], NN)
    right = unpair(right)
    cr[z] = sum(ops[:, i:i + 1] * right[i:i + 1, :] for i in range(RANK))

    c_channel = next(counter)
    for k in by_distance:
        remote(cr.at[z], cr.at[z], c_channel, along_z(k)).start()
    arrived(cr.at[pl.ds(0, nz - 1)], c_channel)
    total = cr[0]
    for k in range(1, nz):
        total = total + cr[k]
    total = total * (1.0 / (2 * nz))
    cfin[...] = total
    coeffs_ref[:, block(c, LANES)] = total
    share_c = remote(cfin, coeffs_ref.at[:, block(c, LANES)], next(counter), partner)
    share_c.start()

    store_basis.wait()
    for ref, channel in sent:
        wait_bytes(ref, send.at[channel])
    share_c.wait()


def body(nx, ny, activations, grad_query, feedback, start_factor):
    tn = nx * ny
    nz = lax.axis_size("dp") // 2
    d = activations.shape[1]
    half, quarter = d // 2, d // 8
    tok, width = grad_query.shape
    vm = pltpu.VMEM
    side = max(nx, ny)
    scratch = [
        vm((RANK, width), F32),
        vm((tok, width), BF16),
        vm((2 * LANES, half), BF16),
        vm((d, width), BF16),
        vm((2, tok, LANES), BF16),
        vm((2, d, LANES), BF16),
        vm((tn, 16, LANES), BF16),
        vm((2 * tn * 16, LANES), BF16),
        vm((4, side, side, RANK, quarter), F32),
        vm((4, side, side, RANK, quarter), F32),
        vm((4, side, RANK, quarter), F32),
        vm((4, side, RANK, quarter), F32),
        vm((2, nz, RANK, LANES), F32),
        vm((nz, RANK, LANES), F32),
        vm((nz, RANK, LANES), F32),
        vm((nz, RANK, LANES), F32),
        vm((nx, ny, nz, 16, LANES), BF16),
        vm((nz, 16, LANES), BF16),
        vm((RANK, d), F32),
        vm((tn * 16, 2 * LANES), F32),
        vm((tn, RANK, 2 * LANES), F32),
        vm((2 * tn, RANK, 2 * LANES), F32),
        vm((nz, RANK, LANES), F32),
        vm((RANK, LANES), F32),
        pltpu.SemaphoreType.DMA((7,)),
        pltpu.SemaphoreType.DMA((CHANNELS,)),
        pltpu.SemaphoreType.DMA((CHANNELS,)),
        pltpu.SemaphoreType.REGULAR((4,)),
    ]
    anywhere = pl.BlockSpec(memory_space=pl.ANY)
    return pl.pallas_call(
        functools.partial(kernel, nx, ny, nz),
        out_shape=(
            jax.ShapeDtypeStruct((RANK, d), F32),
            jax.ShapeDtypeStruct((RANK, width), F32),
        ),
        in_specs=[anywhere] * 4,
        out_specs=(anywhere, pl.BlockSpec(memory_space=pltpu.VMEM)),
        scratch_shapes=scratch,
        compiler_params=pltpu.CompilerParams(
            collective_id=0, has_side_effects=True, vmem_limit_bytes=60 * 1024 * 1024
        ),
    )(start_factor, grad_query, activations, feedback)


def solution(mesh):
    side = 4 if mesh.shape["tensor"] == 16 else 2
    in_specs = (P(("dp", "tensor"), None), P("dp", "tensor"), P("dp", "tensor"), P(None, "tensor"))
    out_specs = (P("tensor", None), P(None, "tensor"))
    return jax.shard_map(
        functools.partial(body, side, mesh.shape["tensor"] // side),
        mesh=mesh, in_specs=in_specs, out_specs=out_specs, check_vma=False,
    )
```

```python
import functools
import itertools

import jax
import jax.numpy as jnp
from jax import lax
from jax.experimental import pallas as pl
from jax.experimental.pallas import tpu as pltpu
from jax.sharding import PartitionSpec as P

EPSILON = 1e-06
MESH = pl.DeviceIdType.MESH
F32, BF16 = jnp.float32, jnp.bfloat16
RANK = 8
LANES = 128
NT = (((1,), (1,)), ((), ()))
NN = (((1,), (0,)), ((), ()))
CHANNELS = 56


def dot(a, b, dims):
    return lax.dot_general(a, b, dims, preferred_element_type=F32)


def pair(value):
    top = value.astype(BF16).astype(F32)
    return jnp.concatenate([top, value - top], axis=0).astype(BF16)


def unpair(value):
    return value[:RANK] + value[RANK:]


def wait_bytes(ref, sem):
    pltpu.make_async_copy(ref, ref, sem).wait()


def hops(k, n):
    return min(k, n - k)


def kernel(
    nx, ny, nz,
    s_hbm, g_hbm, a_hbm, f_hbm,
    basis_hbm, coeffs_ref,
    s_v, g_v, a_v, f_v, gh_v, fh_v,
    psend, precv,
    first, first_in, second, second_in,
    lf, lfr, zs, zr,
    ball, other_half, basis_v,
    qs, qr, cr, cfin,
    local, send, recv, ready,
):
    tn = nx * ny
    half = a_v.shape[1]
    slots = max(nz // 8, 1)
    groups = nz // (2 * slots)
    dp, t = lax.axis_index("dp"), lax.axis_index("tensor")
    z, c = dp // 2, lax.rem(dp, 2)
    o = 1 - c
    x, y = t // ny, lax.rem(t, ny)
    partner = (2 * z + o, t)
    xs = [x] + [lax.rem(x + k, nx) for k in range(1, nx)]
    ys = [y] + [lax.rem(y + k, ny) for k in range(1, ny)]
    around = [z] + [lax.rem(z + k, nz) for k in range(1, nz)]

    def block(index, size):
        return pl.ds(pl.multiple_of(index * size, size), size)

    counter = itertools.count()
    sent = []

    def remote(src, dst, channel, device):
        return pltpu.make_async_remote_copy(
            src_ref=src, dst_ref=dst, send_sem=send.at[channel], recv_sem=recv.at[channel],
            device_id=device, device_id_type=MESH,
        )

    def arrived(ref, channel):
        wait_bytes(ref, recv.at[channel])
        sent.append((ref, channel))

    def along_z(k):
        return (2 * around[k] + c, t)

    def along_x(k):
        return (dp, xs[k] * ny + y)

    def along_y(k):
        return (dp, x * ny + ys[k])

    plane = []
    for dx, dy, dc in itertools.product(range(nx), range(ny), range(2)):
        if dx + dy + dc:
            group = xs[dx] * ny + ys[dy]
            plane.append((hops(dx, nx) + hops(dy, ny), group, (2 * z + o if dc else dp, group)))
    plane.sort(key=lambda entry: -entry[0])
    by_distance = sorted(range(1, nz), key=lambda k: -hops(k, nz))

    load_s = pltpu.make_async_copy(s_hbm, s_v, local.at[0])
    load_g = pltpu.make_async_copy(g_hbm, g_v, local.at[1])
    load_a = pltpu.make_async_copy(a_hbm.at[:, block(c, half)], a_v.at[block(c, LANES), :], local.at[2])
    load_f = pltpu.make_async_copy(f_hbm, f_v, local.at[3])
    load_gh = pltpu.make_async_copy(g_hbm.at[:, block(c, LANES)], gh_v.at[c], local.at[4])
    load_fh = pltpu.make_async_copy(f_hbm.at[:, block(c, LANES)], fh_v.at[c], local.at[5])
    load_s.start()
    load_g.start()

    barrier = pltpu.get_barrier_semaphore()
    beside = sorted({1, nz - 1})
    for _, _, device in plane:
        pl.semaphore_signal(barrier, inc=1, device_id=device, device_id_type=MESH)
    for k in beside:
        pl.semaphore_signal(barrier, inc=1, device_id=along_z(k), device_id_type=MESH)
    for load in (load_a, load_f, load_gh, load_fh):
        load.start()

    reach = [2 ** k for k in range(8) if 2 ** k < nz // 2]

    def tell(step):
        for k in (reach[step], nz - reach[step]):
            pl.semaphore_signal(ready.at[step], inc=1, device_id=along_z(k), device_id_type=MESH)

    load_s.wait()
    s2 = pair(s_v[...])
    load_g.wait()
    p2 = pair(unpair(dot(s2, g_v[...], NT)))
    for k in range(tn):
        psend[k] = p2[:, k * LANES:(k + 1) * LANES]

    pl.semaphore_wait(barrier, len(plane) + len(beside))

    p_channel = next(counter)
    for _, group, device in plane:
        remote(psend.at[group], precv.at[block(c * tn + t, 16), :], p_channel, device).start()
    share_a = remote(a_hbm.at[:, block(o, half)], a_v.at[block(c, LANES), :], next(counter), partner)
    share_a.start()
    tell(0)
    precv[block(c * tn + t, 16), :] = psend[t]

    load_a.wait()
    share_a.wait()
    arrived(precv.at[pl.ds(0, (2 * tn - 1) * 16), :], p_channel)

    def features(k):
        return a_v[:, block(around[k], LANES)]

    def start(r):
        return r[0] * slots if r[1] == 0 else nz - (r[0] + 1) * slots

    def region(r):
        return range(start(r), start(r) + slots)

    def order(r):
        on_x, on_y = (x, nx, xs, along_x), (y, ny, ys, along_y)
        return (on_y, on_x) if r[1] else (on_x, on_y)

    def part_of(r):
        return pl.ds(start(r), slots)

    def index(r):
        return 2 * r[0] + r[1]

    nearest = [(i, side) for i in range(groups) for side in range(2)]
    farthest = [(i, side) for i in reversed(range(groups)) for side in range(2)]

    lhs = jnp.concatenate([precv[:tn * 16, :], precv[tn * 16:, :]], axis=1)
    first_channel, second_channel = {}, {}
    for r in farthest:
        (here, count, _, device), _ = order(r)
        part = dot(lhs, jnp.concatenate([features(k) for k in region(r)], axis=1), NN)
        for gx in range(nx):
            for gy in range(ny):
                g = gx * ny + gy
                i, j = (gy, gx) if r[1] else (gx, gy)
                first[index(r), i, j] = unpair(part[g * 16:(g + 1) * 16])
        first_channel[r] = next(counter)
        others = order(r)[0][2]
        for k in range(1, count):
            remote(first.at[index(r), others[k]], first_in.at[index(r), here], first_channel[r], device(k)).start()
    if len(reach) > 1:
        pl.semaphore_wait(ready.at[0], 2)
        tell(1)

    load_f.wait()
    for h in range(2):
        for k in range(nz):
            at = (h * nz + k) * LANES
            lf[h, k] = unpair(dot(s2, f_v[at:at + LANES, :], NT))
    share_l = remote(lf.at[o], lfr, next(counter), partner)
    share_l.start()

    def pass_on(r):
        (here, count, others, _), (place, size, beyond, device) = order(r)
        arrived(first_in.at[index(r), pl.ds(0, count - 1)], first_channel[r])
        total = first[index(r), here]
        for k in range(1, count):
            total = total + first_in[index(r), others[k]]
        second[index(r)] = total
        second_channel[r] = next(counter)
        for k in range(1, size):
            remote(second.at[index(r), beyond[k]], second_in.at[index(r), place], second_channel[r], device(k)).start()

    z_channel = next(counter)

    def pass_along_z(r):
        _, (place, size, beyond, _) = order(r)
        arrived(second_in.at[index(r), pl.ds(0, size - 1)], second_channel[r])
        total = second[index(r), place]
        for k in range(1, size):
            total = total + second_in[index(r), beyond[k]]
        for i, k in enumerate(region(r)):
            zs[k] = total[:, i * LANES:(i + 1) * LANES] + (lf[c, around[k]] + lfr[around[k]])
        for k in sorted(region(r), key=lambda k: -hops(k, nz)):
            if k:
                remote(zs.at[k], zr.at[k], z_channel, along_z(k)).start()

    ahead = len(farthest) - 2
    for r in farthest[:ahead]:
        pass_on(r)
    if len(reach) > 2:
        pl.semaphore_wait(ready.at[1], 2)
        tell(2)
    share_l.wait()
    for step in range(max(len(reach) - 1, 0), len(reach)):
        pl.semaphore_wait(ready.at[step], 2)
    for r, late in itertools.zip_longest(farthest, farthest[ahead:]):
        pass_along_z(r)
        if late:
            pass_on(late)
    share_g = remote(g_hbm.at[:, block(o, LANES)], gh_v.at[c], next(counter), partner)
    share_g.start()
    share_f = remote(f_hbm.at[:, block(o, LANES)], fh_v.at[c], next(counter), partner)
    share_f.start()
    arrived(zr.at[pl.ds(0, nz - 1)], z_channel)
    total = zs[0]
    for k in range(1, nz):
        total = total + zr[k]

    ball[x, y, 0] = pair(total)
    gather = {r: next(counter) for r in nearest}
    for k in by_distance:
        r = next(r for r in nearest if k in region(r))
        remote(ball.at[x, y, 0], ball.at[x, y, k], gather[r], along_z(nz - k)).start()

    def spread_own(r):
        own = part_of(r)
        if r == nearest[0]:
            if slots > 1:
                arrived(ball.at[x, y, pl.ds(0, slots - 1)], gather[r])
        else:
            arrived(ball.at[x, y, own], gather[r])
        first_channel[r] = next(counter)
        (_, count, _, device), _ = order(r)
        for k in range(1, count):
            remote(ball.at[x, y, own], ball.at[x, y, own], first_channel[r], device(k)).start()

    def spread_line(r):
        own = part_of(r)
        (_, count, _, _), (_, size, _, device) = order(r)
        arrived(ball.at[x, pl.ds(0, count - 1), own], first_channel[r])
        second_channel[r] = next(counter)
        line = ball.at[:, y, own] if r[1] == 0 else ball.at[x, :, own]
        for k in range(1, size):
            remote(line, line, second_channel[r], device(k)).start()

    def product(r):
        own = part_of(r)
        _, (_, size, _, _) = order(r)
        rest = ball.at[:, pl.ds(0, size - 1), own] if r[1] == 0 else ball.at[pl.ds(0, size - 1), :, own]
        arrived(rest, second_channel[r])
        left = jnp.concatenate([ball[:, :, k].reshape(tn * 16, LANES) for k in region(r)], axis=1)
        return dot(left, jnp.concatenate([features(k) for k in region(r)], axis=1), NT)

    for step in range(groups + 2):
        if step < groups:
            spread_own((step, 0))
            spread_own((step, 1))
        if step >= 2:
            spread_line((step - 2, 0))
            spread_line((step - 2, 1))
        if step == groups - 1:
            share_half = remote(ball.at[x, y], other_half, next(counter), partner)
            share_half.start()

    share_half.wait()
    pairs = []
    for h in range(2):
        for k in range(nz):
            slot = lax.rem(k - z + nz, nz)
            pairs.append(jnp.where(c == h, ball[x, y, slot].astype(F32), other_half[slot].astype(F32)))
    v = [unpair(u) for u in pairs]
    row = lax.broadcasted_iota(jnp.int32, (RANK, 1), 0)
    ops = (lax.broadcasted_iota(jnp.int32, (RANK, LANES), 0) == lax.broadcasted_iota(jnp.int32, (RANK, LANES), 1)).astype(F32)
    scale = jnp.zeros((RANK, 1), F32)
    for i in range(RANK):
        own = [jnp.broadcast_to(u[i:i + 1, :], u.shape) for u in v]
        prods = [a * b for a, b in zip(own, v)]
        while len(prods) > 1:
            prods = [a + b for a, b in zip(prods[::2], prods[1::2])]
        dots = jnp.sum(prods[0], axis=1, keepdims=True)
        square = dots[i:i + 1, :] + EPSILON
        scale = jnp.where(row == i, 1.0 / jnp.sqrt(square), scale)
        factor = jnp.where(row > i, dots / square, 0.0)
        v = [u - factor * a for u, a in zip(v, own)]
        ops = ops - factor * jnp.broadcast_to(ops[i:i + 1, :], ops.shape)
    ops = ops * scale
    for k, u in enumerate(v):
        basis_v[:, k * LANES:(k + 1) * LANES] = u * scale
    store_basis = pltpu.make_async_copy(basis_v, basis_hbm, local.at[6])
    store_basis.start()

    load_fh.wait()
    share_f.wait()
    left = jnp.concatenate([u.astype(BF16) for u in pairs], axis=1)
    right = dot(left, fh_v[0], NN) + dot(left, fh_v[1], NN)

    q2 = sum(product(r) for r in nearest)
    for g in range(tn):
        qs[g] = unpair(q2[g * 16:(g + 1) * 16])
    q_channel = next(counter)
    for _, group, device in plane:
        remote(qs.at[group], qr.at[c * tn + t], q_channel, device).start()
    qr[c * tn + t] = qs[t]

    load_gh.wait()
    share_g.wait()
    arrived(qr.at[pl.ds(0, 2 * tn - 1)], q_channel)
    parts = [pair(qr[k] + qr[tn + k]) for k in range(tn)]
    for h in range(2):
        q = jnp.concatenate([u[:, h * LANES:(h + 1) * LANES] for u in parts], axis=1)
        right = right + dot(q, gh_v[h], NN)
    right = unpair(right)
    cr[z] = sum(ops[:, i:i + 1] * right[i:i + 1, :] for i in range(RANK))

    c_channel = next(counter)
    for k in by_distance:
        remote(cr.at[z], cr.at[z], c_channel, along_z(k)).start()
    arrived(cr.at[pl.ds(0, nz - 1)], c_channel)
    total = cr[0]
    for k in range(1, nz):
        total = total + cr[k]
    total = total * (1.0 / (2 * nz))
    cfin[...] = total
    coeffs_ref[:, block(c, LANES)] = total
    share_c = remote(cfin, coeffs_ref.at[:, block(c, LANES)], next(counter), partner)
    share_c.start()

    store_basis.wait()
    for ref, channel in sent:
        wait_bytes(ref, send.at[channel])
    share_c.wait()


def body(nx, ny, activations, grad_query, feedback, start_factor):
    tn = nx * ny
    nz = lax.axis_size("dp") // 2
    d = activations.shape[1]
    half = d // 2
    slots = max(nz // 8, 1)
    regions, part = nz // slots, slots * LANES
    tok, width = grad_query.shape
    vm = pltpu.VMEM
    side = max(nx, ny)
    scratch = [
        vm((RANK, width), F32),
        vm((tok, width), BF16),
        vm((2 * LANES, half), BF16),
        vm((d, width), BF16),
        vm((2, tok, LANES), BF16),
        vm((2, d, LANES), BF16),
        vm((tn, 16, LANES), BF16),
        vm((2 * tn * 16, LANES), BF16),
        vm((regions, side, side, RANK, part), F32),
        vm((regions, side, side, RANK, part), F32),
        vm((regions, side, RANK, part), F32),
        vm((regions, side, RANK, part), F32),
        vm((2, nz, RANK, LANES), F32),
        vm((nz, RANK, LANES), F32),
        vm((nz, RANK, LANES), F32),
        vm((nz, RANK, LANES), F32),
        vm((nx, ny, nz, 16, LANES), BF16),
        vm((nz, 16, LANES), BF16),
        vm((RANK, d), F32),
        vm((tn, RANK, 2 * LANES), F32),
        vm((2 * tn, RANK, 2 * LANES), F32),
        vm((nz, RANK, LANES), F32),
        vm((RANK, LANES), F32),
        pltpu.SemaphoreType.DMA((7,)),
        pltpu.SemaphoreType.DMA((CHANNELS,)),
        pltpu.SemaphoreType.DMA((CHANNELS,)),
        pltpu.SemaphoreType.REGULAR((4,)),
    ]
    anywhere = pl.BlockSpec(memory_space=pl.ANY)
    return pl.pallas_call(
        functools.partial(kernel, nx, ny, nz),
        out_shape=(
            jax.ShapeDtypeStruct((RANK, d), F32),
            jax.ShapeDtypeStruct((RANK, width), F32),
        ),
        in_specs=[anywhere] * 4,
        out_specs=(anywhere, pl.BlockSpec(memory_space=pltpu.VMEM)),
        scratch_shapes=scratch,
        compiler_params=pltpu.CompilerParams(
            collective_id=0, has_side_effects=True, vmem_limit_bytes=54600 * 1024
        ),
    )(start_factor, grad_query, activations, feedback)


def solution(mesh):
    side = 4 if mesh.shape["tensor"] == 16 else 2
    in_specs = (P(("dp", "tensor"), None), P("dp", "tensor"), P("dp", "tensor"), P(None, "tensor"))
    out_specs = (P("tensor", None), P(None, "tensor"))
    return jax.shard_map(
        functools.partial(body, side, mesh.shape["tensor"] // side),
        mesh=mesh, in_specs=in_specs, out_specs=out_specs, check_vma=False,
    )
```

```python
import functools
import itertools

import jax
import jax.numpy as jnp
from jax import lax
from jax.experimental import pallas as pl
from jax.experimental.pallas import tpu as pltpu
from jax.sharding import PartitionSpec as P

EPSILON = 1e-06
MESH = pl.DeviceIdType.MESH
F32, BF16 = jnp.float32, jnp.bfloat16
RANK = 8
LANES = 128
NT = (((1,), (1,)), ((), ()))
NN = (((1,), (0,)), ((), ()))
CHANNELS = 56


def dot(a, b, dims):
    return lax.dot_general(a, b, dims, preferred_element_type=F32)


def pair(value):
    top = value.astype(BF16).astype(F32)
    return jnp.concatenate([top, value - top], axis=0).astype(BF16)


def unpair(value):
    return value[:RANK] + value[RANK:]


def wait_bytes(ref, sem):
    pltpu.make_async_copy(ref, ref, sem).wait()


def hops(k, n):
    return min(k, n - k)


def kernel(
    nx, ny, nz,
    s_hbm, g_hbm, a_hbm, f_hbm,
    basis_hbm, coeffs_ref,
    s_v, g_v, a_v, f_v, gh_v, fh_v,
    psend, precv,
    first, first_in, second, second_in,
    lf, lfr, zs, zr,
    ball, other_half, basis_v,
    qs, qr, cr, cfin,
    local, send, recv, ready,
):
    tn = nx * ny
    half = a_v.shape[1]
    slots = max(nz // 8, 1)
    groups = nz // (2 * slots)
    dp, t = lax.axis_index("dp"), lax.axis_index("tensor")
    z, c = dp // 2, lax.rem(dp, 2)
    o = 1 - c
    x, y = t // ny, lax.rem(t, ny)
    partner = (2 * z + o, t)
    xs = [x] + [lax.rem(x + k, nx) for k in range(1, nx)]
    ys = [y] + [lax.rem(y + k, ny) for k in range(1, ny)]
    around = [z] + [lax.rem(z + k, nz) for k in range(1, nz)]

    def block(index, size):
        return pl.ds(pl.multiple_of(index * size, size), size)

    counter = itertools.count()
    sent = []

    def remote(src, dst, channel, device):
        return pltpu.make_async_remote_copy(
            src_ref=src, dst_ref=dst, send_sem=send.at[channel], recv_sem=recv.at[channel],
            device_id=device, device_id_type=MESH,
        )

    def arrived(ref, channel):
        wait_bytes(ref, recv.at[channel])
        sent.append((ref, channel))

    def along_z(k):
        return (2 * around[k] + c, t)

    def along_x(k):
        return (dp, xs[k] * ny + y)

    def along_y(k):
        return (dp, x * ny + ys[k])

    plane = []
    for dx, dy, dc in itertools.product(range(nx), range(ny), range(2)):
        if dx + dy + dc:
            group = xs[dx] * ny + ys[dy]
            plane.append((hops(dx, nx) + hops(dy, ny), group, (2 * z + o if dc else dp, group), not dc))
    plane.sort(key=lambda entry: -entry[0])
    by_distance = sorted(range(1, nz), key=lambda k: -hops(k, nz))

    load_s = pltpu.make_async_copy(s_hbm, s_v, local.at[0])
    load_g = pltpu.make_async_copy(g_hbm, g_v, local.at[1])
    load_a = pltpu.make_async_copy(a_hbm.at[:, block(c, half)], a_v.at[block(c, LANES), :], local.at[2])
    load_f = pltpu.make_async_copy(f_hbm, f_v, local.at[3])
    load_gh = pltpu.make_async_copy(g_hbm.at[:, block(c, LANES)], gh_v.at[c], local.at[4])
    load_fh = pltpu.make_async_copy(f_hbm.at[:, block(c, LANES)], fh_v.at[c], local.at[5])
    load_s.start()
    load_g.start()

    barrier = pltpu.get_barrier_semaphore()
    beside = sorted({1, nz - 1})
    for _, _, device, _ in plane:
        pl.semaphore_signal(barrier, inc=1, device_id=device, device_id_type=MESH)
    for k in beside:
        pl.semaphore_signal(barrier, inc=1, device_id=along_z(k), device_id_type=MESH)
    for load in (load_a, load_f, load_gh, load_fh):
        load.start()

    reach = [2 ** k for k in range(8) if 2 ** k < nz // 2]

    def tell(step):
        for k in (reach[step], nz - reach[step]):
            pl.semaphore_signal(ready.at[step], inc=1, device_id=along_z(k), device_id_type=MESH)

    load_s.wait()
    s2 = pair(s_v[...])
    load_g.wait()
    p2 = pair(unpair(dot(s2, g_v[...], NT)))
    for k in range(tn):
        psend[k] = p2[:, k * LANES:(k + 1) * LANES]

    pl.semaphore_wait(barrier, len(plane) + len(beside))

    p_channel = next(counter)
    for _, group, device, _ in plane:
        remote(psend.at[group], precv.at[block(c * tn + t, 16), :], p_channel, device).start()
    share_a = remote(a_hbm.at[:, block(o, half)], a_v.at[block(c, LANES), :], next(counter), partner)
    share_a.start()
    tell(0)
    precv[block(c * tn + t, 16), :] = psend[t]

    load_a.wait()
    share_a.wait()
    arrived(precv.at[pl.ds(0, (2 * tn - 1) * 16), :], p_channel)

    def features(k):
        return a_v[:, block(around[k], LANES)]

    def start(r):
        return r[0] * slots if r[1] == 0 else nz - (r[0] + 1) * slots

    def region(r):
        return range(start(r), start(r) + slots)

    def order(r):
        on_x, on_y = (x, nx, xs, along_x), (y, ny, ys, along_y)
        return (on_y, on_x) if r[1] else (on_x, on_y)

    def part_of(r):
        return pl.ds(start(r), slots)

    def index(r):
        return 2 * r[0] + r[1]

    nearest = [(i, side) for i in range(groups) for side in range(2)]
    farthest = [(i, side) for i in reversed(range(groups)) for side in range(2)]

    lhs = jnp.concatenate([precv[:tn * 16, :], precv[tn * 16:, :]], axis=1)
    first_channel, second_channel = {}, {}
    for r in farthest:
        (here, count, _, device), _ = order(r)
        part = dot(lhs, jnp.concatenate([features(k) for k in region(r)], axis=1), NN)
        for gx in range(nx):
            for gy in range(ny):
                g = gx * ny + gy
                i, j = (gy, gx) if r[1] else (gx, gy)
                first[index(r), i, j] = unpair(part[g * 16:(g + 1) * 16])
        first_channel[r] = next(counter)
        others = order(r)[0][2]
        for k in range(1, count):
            remote(first.at[index(r), others[k]], first_in.at[index(r), here], first_channel[r], device(k)).start()
    if len(reach) > 1:
        pl.semaphore_wait(ready.at[0], 2)
        tell(1)

    load_f.wait()
    for h in range(2):
        for k in range(nz):
            at = (h * nz + k) * LANES
            lf[h, k] = unpair(dot(s2, f_v[at:at + LANES, :], NT))
    share_l = remote(lf.at[o], lfr, next(counter), partner)
    share_l.start()

    def pass_on(r):
        (here, count, others, _), (place, size, beyond, device) = order(r)
        arrived(first_in.at[index(r), pl.ds(0, count - 1)], first_channel[r])
        total = first[index(r), here]
        for k in range(1, count):
            total = total + first_in[index(r), others[k]]
        second[index(r)] = total
        second_channel[r] = next(counter)
        for k in range(1, size):
            remote(second.at[index(r), beyond[k]], second_in.at[index(r), place], second_channel[r], device(k)).start()

    z_channel = next(counter)

    def pass_along_z(r):
        _, (place, size, beyond, _) = order(r)
        arrived(second_in.at[index(r), pl.ds(0, size - 1)], second_channel[r])
        total = second[index(r), place]
        for k in range(1, size):
            total = total + second_in[index(r), beyond[k]]
        for i, k in enumerate(region(r)):
            zs[k] = total[:, i * LANES:(i + 1) * LANES] + (lf[c, around[k]] + lfr[around[k]])
        for k in sorted(region(r), key=lambda k: -hops(k, nz)):
            if k:
                remote(zs.at[k], zr.at[k], z_channel, along_z(k)).start()

    ahead = len(farthest) - 2
    for r in farthest[:ahead]:
        pass_on(r)
    if len(reach) > 2:
        pl.semaphore_wait(ready.at[1], 2)
        tell(2)
    share_l.wait()
    for step in range(max(len(reach) - 1, 0), len(reach)):
        pl.semaphore_wait(ready.at[step], 2)
    for r, late in itertools.zip_longest(farthest, farthest[ahead:]):
        pass_along_z(r)
        if late:
            pass_on(late)
    share_g = remote(g_hbm.at[:, block(o, LANES)], gh_v.at[c], next(counter), partner)
    share_g.start()
    share_f = remote(f_hbm.at[:, block(o, LANES)], fh_v.at[c], next(counter), partner)
    share_f.start()
    arrived(zr.at[pl.ds(0, nz - 1)], z_channel)
    total = zs[0]
    for k in range(1, nz):
        total = total + zr[k]

    ball[x, y, 0] = pair(total)
    gather = {r: next(counter) for r in nearest}
    for k in by_distance:
        r = next(r for r in nearest if k in region(r))
        remote(ball.at[x, y, 0], ball.at[x, y, k], gather[r], along_z(nz - k)).start()

    def spread_own(r):
        own = part_of(r)
        if r == nearest[0]:
            if slots > 1:
                arrived(ball.at[x, y, pl.ds(0, slots - 1)], gather[r])
        else:
            arrived(ball.at[x, y, own], gather[r])
        first_channel[r] = next(counter)
        (_, count, _, device), _ = order(r)
        for k in range(1, count):
            remote(ball.at[x, y, own], ball.at[x, y, own], first_channel[r], device(k)).start()

    def spread_line(r):
        own = part_of(r)
        (_, count, _, _), (_, size, _, device) = order(r)
        arrived(ball.at[x, pl.ds(0, count - 1), own], first_channel[r])
        second_channel[r] = next(counter)
        line = ball.at[:, y, own] if r[1] == 0 else ball.at[x, :, own]
        for k in range(1, size):
            remote(line, line, second_channel[r], device(k)).start()

    def columns(slots_of):
        return jnp.concatenate([features(k) for k in slots_of], axis=1)

    def lines(slots_of):
        return jnp.concatenate([ball[:, :, k].reshape(tn * 16, LANES) for k in slots_of], axis=1)

    def product(r):
        own = part_of(r)
        _, (_, size, _, _) = order(r)
        rest = ball.at[:, pl.ds(0, size - 1), own] if r[1] == 0 else ball.at[pl.ds(0, size - 1), :, own]
        arrived(rest, second_channel[r])
        return dot(lines(region(r)), columns(region(r)), NT)

    last = groups - 1
    opposite = range(start((last, 0)), start((last, 1)) + slots)
    for step in range(last):
        spread_own((step, 0))
        spread_own((step, 1))
        if step >= 2:
            spread_line((step - 2, 0))
            spread_line((step - 2, 1))
    for side in range(2):
        arrived(ball.at[x, y, part_of((last, side))], gather[last, side])
    straight = next(counter)
    far = pl.ds(opposite[0], len(opposite))
    for _, _, device, same in plane:
        if same:
            remote(ball.at[x, y, far], ball.at[x, y, far], straight, device).start()
    share_half = remote(ball.at[x, y], other_half, next(counter), partner)
    share_half.start()
    for step in range(max(last - 2, 0), last):
        spread_line((step, 0))
        spread_line((step, 1))

    share_half.wait()
    pairs = []
    for h in range(2):
        for k in range(nz):
            slot = lax.rem(k - z + nz, nz)
            pairs.append(jnp.where(c == h, ball[x, y, slot].astype(F32), other_half[slot].astype(F32)))
    v = [unpair(u) for u in pairs]
    row = lax.broadcasted_iota(jnp.int32, (RANK, 1), 0)
    ops = (lax.broadcasted_iota(jnp.int32, (RANK, LANES), 0) == lax.broadcasted_iota(jnp.int32, (RANK, LANES), 1)).astype(F32)
    scale = jnp.zeros((RANK, 1), F32)
    for i in range(RANK):
        own = [jnp.broadcast_to(u[i:i + 1, :], u.shape) for u in v]
        prods = [a * b for a, b in zip(own, v)]
        while len(prods) > 1:
            prods = [a + b for a, b in zip(prods[::2], prods[1::2])]
        dots = jnp.sum(prods[0], axis=1, keepdims=True)
        square = dots[i:i + 1, :] + EPSILON
        scale = jnp.where(row == i, 1.0 / jnp.sqrt(square), scale)
        factor = jnp.where(row > i, dots / square, 0.0)
        v = [u - factor * a for u, a in zip(v, own)]
        ops = ops - factor * jnp.broadcast_to(ops[i:i + 1, :], ops.shape)
    ops = ops * scale
    for k, u in enumerate(v):
        basis_v[:, k * LANES:(k + 1) * LANES] = u * scale
    store_basis = pltpu.make_async_copy(basis_v, basis_hbm, local.at[6])
    store_basis.start()

    load_fh.wait()
    share_f.wait()
    left = jnp.concatenate([u.astype(BF16) for u in pairs], axis=1)
    right = dot(left, fh_v[0], NN) + dot(left, fh_v[1], NN)

    q2 = sum(product(r) for r in nearest[:-2])
    arrived(ball.at[pl.ds(0, len(opposite)), 0, pl.ds(0, tn - 1)], straight)
    q2 = q2 + dot(lines(opposite), columns(opposite), NT)
    for g in range(tn):
        qs[g] = unpair(q2[g * 16:(g + 1) * 16])
    q_channel = next(counter)
    for _, group, device, _ in plane:
        remote(qs.at[group], qr.at[c * tn + t], q_channel, device).start()
    qr[c * tn + t] = qs[t]

    load_gh.wait()
    share_g.wait()
    arrived(qr.at[pl.ds(0, 2 * tn - 1)], q_channel)
    parts = [pair(qr[k] + qr[tn + k]) for k in range(tn)]
    for h in range(2):
        q = jnp.concatenate([u[:, h * LANES:(h + 1) * LANES] for u in parts], axis=1)
        right = right + dot(q, gh_v[h], NN)
    right = unpair(right)
    cr[z] = sum(ops[:, i:i + 1] * right[i:i + 1, :] for i in range(RANK))

    c_channel = next(counter)
    for k in by_distance:
        remote(cr.at[z], cr.at[z], c_channel, along_z(k)).start()
    arrived(cr.at[pl.ds(0, nz - 1)], c_channel)
    total = cr[0]
    for k in range(1, nz):
        total = total + cr[k]
    total = total * (1.0 / (2 * nz))
    cfin[...] = total
    coeffs_ref[:, block(c, LANES)] = total
    share_c = remote(cfin, coeffs_ref.at[:, block(c, LANES)], next(counter), partner)
    share_c.start()

    store_basis.wait()
    for ref, channel in sent:
        wait_bytes(ref, send.at[channel])
    share_c.wait()


def body(nx, ny, activations, grad_query, feedback, start_factor):
    tn = nx * ny
    nz = lax.axis_size("dp") // 2
    d = activations.shape[1]
    half = d // 2
    slots = max(nz // 8, 1)
    regions, part = nz // slots, slots * LANES
    tok, width = grad_query.shape
    vm = pltpu.VMEM
    side = max(nx, ny)
    scratch = [
        vm((RANK, width), F32),
        vm((tok, width), BF16),
        vm((2 * LANES, half), BF16),
        vm((d, width), BF16),
        vm((2, tok, LANES), BF16),
        vm((2, d, LANES), BF16),
        vm((tn, 16, LANES), BF16),
        vm((2 * tn * 16, LANES), BF16),
        vm((regions, side, side, RANK, part), F32),
        vm((regions, side, side, RANK, part), F32),
        vm((regions, side, RANK, part), F32),
        vm((regions, side, RANK, part), F32),
        vm((2, nz, RANK, LANES), F32),
        vm((nz, RANK, LANES), F32),
        vm((nz, RANK, LANES), F32),
        vm((nz, RANK, LANES), F32),
        vm((nx, ny, nz, 16, LANES), BF16),
        vm((nz, 16, LANES), BF16),
        vm((RANK, d), F32),
        vm((tn, RANK, 2 * LANES), F32),
        vm((2 * tn, RANK, 2 * LANES), F32),
        vm((nz, RANK, LANES), F32),
        vm((RANK, LANES), F32),
        pltpu.SemaphoreType.DMA((7,)),
        pltpu.SemaphoreType.DMA((CHANNELS,)),
        pltpu.SemaphoreType.DMA((CHANNELS,)),
        pltpu.SemaphoreType.REGULAR((4,)),
    ]
    anywhere = pl.BlockSpec(memory_space=pl.ANY)
    return pl.pallas_call(
        functools.partial(kernel, nx, ny, nz),
        out_shape=(
            jax.ShapeDtypeStruct((RANK, d), F32),
            jax.ShapeDtypeStruct((RANK, width), F32),
        ),
        in_specs=[anywhere] * 4,
        out_specs=(anywhere, pl.BlockSpec(memory_space=pltpu.VMEM)),
        scratch_shapes=scratch,
        compiler_params=pltpu.CompilerParams(
            collective_id=0, has_side_effects=True, vmem_limit_bytes=54600 * 1024
        ),
    )(start_factor, grad_query, activations, feedback)


def solution(mesh):
    side = 4 if mesh.shape["tensor"] == 16 else 2
    in_specs = (P(("dp", "tensor"), None), P("dp", "tensor"), P("dp", "tensor"), P(None, "tensor"))
    out_specs = (P("tensor", None), P(None, "tensor"))
    return jax.shard_map(
        functools.partial(body, side, mesh.shape["tensor"] // side),
        mesh=mesh, in_specs=in_specs, out_specs=out_specs, check_vma=False,
    )
```

```python
import functools
import itertools

import jax
import jax.numpy as jnp
from jax import lax
from jax.experimental import pallas as pl
from jax.experimental.pallas import tpu as pltpu
from jax.sharding import PartitionSpec as P

EPSILON = 1e-06
MESH = pl.DeviceIdType.MESH
F32, BF16 = jnp.float32, jnp.bfloat16
RANK = 8
LANES = 128
NT = (((1,), (1,)), ((), ()))
NN = (((1,), (0,)), ((), ()))
CHANNELS = 56


def dot(a, b, dims):
    return lax.dot_general(a, b, dims, preferred_element_type=F32)


def pair(value):
    top = value.astype(BF16).astype(F32)
    return jnp.concatenate([top, value - top], axis=0).astype(BF16)


def unpair(value):
    return value[:RANK] + value[RANK:]


def wait_bytes(ref, sem):
    pltpu.make_async_copy(ref, ref, sem).wait()


def hops(k, n):
    return min(k, n - k)


def kernel(
    nx, ny, nz,
    s_hbm, g_hbm, a_hbm, f_hbm,
    basis_hbm, coeffs_ref,
    s_v, g_v, a_v, f_v, gh_v, fh_v,
    psend, precv,
    first, first_in, second, second_in,
    lf, lfr, zs, zr,
    ball, other_half, basis_v,
    qs, qr, cr, cfin,
    local, send, recv, ready,
):
    tn = nx * ny
    half = a_v.shape[1]
    slots = max(nz // 8, 1)
    groups = nz // (2 * slots)
    dp, t = lax.axis_index("dp"), lax.axis_index("tensor")
    z, c = dp // 2, lax.rem(dp, 2)
    o = 1 - c
    x, y = t // ny, lax.rem(t, ny)
    partner = (2 * z + o, t)
    xs = [x] + [lax.rem(x + k, nx) for k in range(1, nx)]
    ys = [y] + [lax.rem(y + k, ny) for k in range(1, ny)]
    around = [z] + [lax.rem(z + k, nz) for k in range(1, nz)]

    def block(index, size):
        return pl.ds(pl.multiple_of(index * size, size), size)

    counter = itertools.count()
    sent = []

    def remote(src, dst, channel, device):
        return pltpu.make_async_remote_copy(
            src_ref=src, dst_ref=dst, send_sem=send.at[channel], recv_sem=recv.at[channel],
            device_id=device, device_id_type=MESH,
        )

    def arrived(ref, channel):
        wait_bytes(ref, recv.at[channel])
        sent.append((ref, channel))

    def along_z(k):
        return (2 * around[k] + c, t)

    def along_x(k):
        return (dp, xs[k] * ny + y)

    def along_y(k):
        return (dp, x * ny + ys[k])

    plane = []
    for dx, dy, dc in itertools.product(range(nx), range(ny), range(2)):
        if dx + dy + dc:
            group = xs[dx] * ny + ys[dy]
            plane.append((hops(dx, nx) + hops(dy, ny), group, (2 * z + o if dc else dp, group), not dc))
    plane.sort(key=lambda entry: -entry[0])
    by_distance = sorted(range(1, nz), key=lambda k: -hops(k, nz))

    load_s = pltpu.make_async_copy(s_hbm, s_v, local.at[0])
    load_g = pltpu.make_async_copy(g_hbm, g_v, local.at[1])
    load_a = pltpu.make_async_copy(a_hbm.at[:, block(c, half)], a_v.at[block(c, LANES), :], local.at[2])
    load_f = pltpu.make_async_copy(f_hbm, f_v, local.at[3])
    load_gh = pltpu.make_async_copy(g_hbm.at[:, block(c, LANES)], gh_v.at[c], local.at[4])
    load_fh = pltpu.make_async_copy(f_hbm.at[:, block(c, LANES)], fh_v.at[c], local.at[5])
    barrier = pltpu.get_barrier_semaphore()
    beside = sorted({1, nz - 1})
    for _, _, device, _ in plane:
        pl.semaphore_signal(barrier, inc=1, device_id=device, device_id_type=MESH)
    for k in beside:
        pl.semaphore_signal(barrier, inc=1, device_id=along_z(k), device_id_type=MESH)
    for load in (load_s, load_g, load_a, load_f, load_gh, load_fh):
        load.start()

    reach = [2 ** k for k in range(8) if 2 ** k < nz // 2]

    def tell(step):
        for k in (reach[step], nz - reach[step]):
            pl.semaphore_signal(ready.at[step], inc=1, device_id=along_z(k), device_id_type=MESH)

    load_s.wait()
    s2 = pair(s_v[...])
    load_g.wait()
    p2 = pair(unpair(dot(s2, g_v[...], NT)))
    for k in range(tn):
        psend[k] = p2[:, k * LANES:(k + 1) * LANES]

    pl.semaphore_wait(barrier, len(plane) + len(beside))

    p_channel = next(counter)
    for _, group, device, _ in plane:
        remote(psend.at[group], precv.at[block(c * tn + t, 16), :], p_channel, device).start()
    share_a = remote(a_hbm.at[:, block(o, half)], a_v.at[block(c, LANES), :], next(counter), partner)
    share_a.start()
    tell(0)
    precv[block(c * tn + t, 16), :] = psend[t]

    load_a.wait()
    share_a.wait()
    arrived(precv.at[pl.ds(0, (2 * tn - 1) * 16), :], p_channel)

    def features(k):
        return a_v[:, block(around[k], LANES)]

    def start(r):
        return r[0] * slots if r[1] == 0 else nz - (r[0] + 1) * slots

    def region(r):
        return range(start(r), start(r) + slots)

    def order(r):
        on_x, on_y = (x, nx, xs, along_x), (y, ny, ys, along_y)
        return (on_y, on_x) if r[1] else (on_x, on_y)

    def part_of(r):
        return pl.ds(start(r), slots)

    wide = first.shape[-1] // LANES

    def wide_region(r):
        begin = r[0] * wide if r[1] == 0 else nz - (r[0] + 1) * wide
        return range(begin, begin + wide)

    def index(r):
        return 2 * r[0] + r[1]

    nearest = [(i, side) for i in range(groups) for side in range(2)]
    farthest = [(i, side) for i in reversed(range(nz // (2 * wide))) for side in range(2)]

    lhs = jnp.concatenate([precv[:tn * 16, :], precv[tn * 16:, :]], axis=1)
    first_channel, second_channel = {}, {}
    for r in farthest:
        (here, count, _, device), _ = order(r)
        part = dot(lhs, jnp.concatenate([features(k) for k in wide_region(r)], axis=1), NN)
        for gx in range(nx):
            for gy in range(ny):
                g = gx * ny + gy
                i, j = (gy, gx) if r[1] else (gx, gy)
                first[index(r), i, j] = unpair(part[g * 16:(g + 1) * 16])
        first_channel[r] = next(counter)
        others = order(r)[0][2]
        for k in range(1, count):
            remote(first.at[index(r), others[k]], first_in.at[index(r), here], first_channel[r], device(k)).start()
    if len(reach) > 1:
        pl.semaphore_wait(ready.at[0], 2)
        tell(1)

    load_f.wait()
    for h in range(2):
        for k in range(nz):
            at = (h * nz + k) * LANES
            lf[h, k] = unpair(dot(s2, f_v[at:at + LANES, :], NT))
    share_l = remote(lf.at[o], lfr, next(counter), partner)
    share_l.start()

    def pass_on(r):
        (here, count, others, _), (place, size, beyond, device) = order(r)
        arrived(first_in.at[index(r), pl.ds(0, count - 1)], first_channel[r])
        total = first[index(r), here]
        for k in range(1, count):
            total = total + first_in[index(r), others[k]]
        second[index(r)] = total
        second_channel[r] = next(counter)
        for k in range(1, size):
            remote(second.at[index(r), beyond[k]], second_in.at[index(r), place], second_channel[r], device(k)).start()

    z_channel = next(counter)

    def pass_along_z(r):
        _, (place, size, beyond, _) = order(r)
        arrived(second_in.at[index(r), pl.ds(0, size - 1)], second_channel[r])
        total = second[index(r), place]
        for k in range(1, size):
            total = total + second_in[index(r), beyond[k]]
        for i, k in enumerate(wide_region(r)):
            zs[k] = total[:, i * LANES:(i + 1) * LANES] + (lf[c, around[k]] + lfr[around[k]])
        for k in sorted(wide_region(r), key=lambda k: -hops(k, nz)):
            if k:
                remote(zs.at[k], zr.at[k], z_channel, along_z(k)).start()

    ahead = len(farthest) - 2
    for r in farthest[:ahead]:
        pass_on(r)
    if len(reach) > 2:
        pl.semaphore_wait(ready.at[1], 2)
        tell(2)
    share_l.wait()
    for step in range(max(len(reach) - 1, 0), len(reach)):
        pl.semaphore_wait(ready.at[step], 2)
    for r, late in itertools.zip_longest(farthest, farthest[ahead:]):
        pass_along_z(r)
        if late:
            pass_on(late)
    share_g = remote(g_hbm.at[:, block(o, LANES)], gh_v.at[c], next(counter), partner)
    share_g.start()
    share_f = remote(f_hbm.at[:, block(o, LANES)], fh_v.at[c], next(counter), partner)
    share_f.start()
    arrived(zr.at[pl.ds(0, nz - 1)], z_channel)
    total = zs[0]
    for k in range(1, nz):
        total = total + zr[k]

    ball[x, y, 0] = pair(total)
    gather = {r: next(counter) for r in nearest}
    for k in by_distance:
        r = next(r for r in nearest if k in region(r))
        remote(ball.at[x, y, 0], ball.at[x, y, k], gather[r], along_z(nz - k)).start()

    def spread_own(r):
        own = part_of(r)
        if r == nearest[0]:
            if slots > 1:
                arrived(ball.at[x, y, pl.ds(0, slots - 1)], gather[r])
        else:
            arrived(ball.at[x, y, own], gather[r])
        first_channel[r] = next(counter)
        (_, count, _, device), _ = order(r)
        for k in range(1, count):
            remote(ball.at[x, y, own], ball.at[x, y, own], first_channel[r], device(k)).start()

    def spread_line(r):
        own = part_of(r)
        (_, count, _, _), (_, size, _, device) = order(r)
        arrived(ball.at[x, pl.ds(0, count - 1), own], first_channel[r])
        second_channel[r] = next(counter)
        line = ball.at[:, y, own] if r[1] == 0 else ball.at[x, :, own]
        for k in range(1, size):
            remote(line, line, second_channel[r], device(k)).start()

    def columns(slots_of):
        return jnp.concatenate([features(k) for k in slots_of], axis=1)

    def lines(slots_of):
        return jnp.concatenate([ball[:, :, k].reshape(tn * 16, LANES) for k in slots_of], axis=1)

    def product(r):
        own = part_of(r)
        _, (_, size, _, _) = order(r)
        rest = ball.at[:, pl.ds(0, size - 1), own] if r[1] == 0 else ball.at[pl.ds(0, size - 1), :, own]
        arrived(rest, second_channel[r])
        return dot(lines(region(r)), columns(region(r)), NT)

    last = groups - 1
    opposite = range(start((last, 0)), start((last, 1)) + slots)
    for step in range(last):
        spread_own((step, 0))
        spread_own((step, 1))
    for side in range(2):
        arrived(ball.at[x, y, part_of((last, side))], gather[last, side])
    straight = next(counter)
    far = pl.ds(opposite[0], len(opposite))
    for _, _, device, same in plane:
        if same:
            remote(ball.at[x, y, far], ball.at[x, y, far], straight, device).start()
    share_half = remote(ball.at[x, y], other_half, next(counter), partner)
    share_half.start()
    for step in range(last):
        spread_line((step, 0))
        spread_line((step, 1))

    share_half.wait()
    pairs = []
    for h in range(2):
        for k in range(nz):
            slot = lax.rem(k - z + nz, nz)
            pairs.append(jnp.where(c == h, ball[x, y, slot].astype(F32), other_half[slot].astype(F32)))
    v = [unpair(u) for u in pairs]
    row = lax.broadcasted_iota(jnp.int32, (RANK, 1), 0)
    ops = (lax.broadcasted_iota(jnp.int32, (RANK, LANES), 0) == lax.broadcasted_iota(jnp.int32, (RANK, LANES), 1)).astype(F32)
    scale = jnp.zeros((RANK, 1), F32)
    for i in range(RANK):
        own = [jnp.broadcast_to(u[i:i + 1, :], u.shape) for u in v]
        prods = [a * b for a, b in zip(own, v)]
        while len(prods) > 1:
            prods = [a + b for a, b in zip(prods[::2], prods[1::2])]
        dots = jnp.sum(prods[0], axis=1, keepdims=True)
        square = dots[i:i + 1, :] + EPSILON
        scale = jnp.where(row == i, 1.0 / jnp.sqrt(square), scale)
        factor = jnp.where(row > i, dots / square, 0.0)
        v = [u - factor * a for u, a in zip(v, own)]
        ops = ops - factor * jnp.broadcast_to(ops[i:i + 1, :], ops.shape)
    ops = ops * scale
    for k, u in enumerate(v):
        basis_v[:, k * LANES:(k + 1) * LANES] = u * scale
    store_basis = pltpu.make_async_copy(basis_v, basis_hbm, local.at[6])
    store_basis.start()

    load_fh.wait()
    share_f.wait()
    left = jnp.concatenate([u.astype(BF16) for u in pairs], axis=1)
    right = dot(left, fh_v[0], NN) + dot(left, fh_v[1], NN)

    q2 = sum(product(r) for r in nearest[:-2])
    arrived(ball.at[pl.ds(0, len(opposite)), 0, pl.ds(0, tn - 1)], straight)
    q2 = q2 + dot(lines(opposite), columns(opposite), NT)
    for g in range(tn):
        qs[g] = unpair(q2[g * 16:(g + 1) * 16])
    q_channel = next(counter)
    for _, group, device, _ in plane:
        remote(qs.at[group], qr.at[c * tn + t], q_channel, device).start()
    qr[c * tn + t] = qs[t]

    load_gh.wait()
    share_g.wait()
    arrived(qr.at[pl.ds(0, 2 * tn - 1)], q_channel)
    parts = [pair(qr[k] + qr[tn + k]) for k in range(tn)]
    for h in range(2):
        q = jnp.concatenate([u[:, h * LANES:(h + 1) * LANES] for u in parts], axis=1)
        right = right + dot(q, gh_v[h], NN)
    right = unpair(right)
    cr[z] = sum(ops[:, i:i + 1] * right[i:i + 1, :] for i in range(RANK))

    c_channel = next(counter)
    for k in by_distance:
        remote(cr.at[z], cr.at[z], c_channel, along_z(k)).start()
    store_basis.wait()
    for ref, channel in sent:
        wait_bytes(ref, send.at[channel])
    wait_bytes(cr.at[pl.ds(0, nz - 1)], recv.at[c_channel])
    total = cr[0]
    for k in range(1, nz):
        total = total + cr[k]
    total = total * (1.0 / (2 * nz))
    cfin[...] = total
    coeffs_ref[:, block(c, LANES)] = total
    share_c = remote(cfin, coeffs_ref.at[:, block(c, LANES)], next(counter), partner)
    share_c.start()

    wait_bytes(cr.at[pl.ds(0, nz - 1)], send.at[c_channel])
    share_c.wait()


def body(nx, ny, activations, grad_query, feedback, start_factor):
    tn = nx * ny
    nz = lax.axis_size("dp") // 2
    d = activations.shape[1]
    half = d // 2
    wide = max(nz // 4, 1)
    regions, part = nz // wide, wide * LANES
    tok, width = grad_query.shape
    vm = pltpu.VMEM
    side = max(nx, ny)
    scratch = [
        vm((RANK, width), F32),
        vm((tok, width), BF16),
        vm((2 * LANES, half), BF16),
        vm((d, width), BF16),
        vm((2, tok, LANES), BF16),
        vm((2, d, LANES), BF16),
        vm((tn, 16, LANES), BF16),
        vm((2 * tn * 16, LANES), BF16),
        vm((regions, side, side, RANK, part), F32),
        vm((regions, side, side, RANK, part), F32),
        vm((regions, side, RANK, part), F32),
        vm((regions, side, RANK, part), F32),
        vm((2, nz, RANK, LANES), F32),
        vm((nz, RANK, LANES), F32),
        vm((nz, RANK, LANES), F32),
        vm((nz, RANK, LANES), F32),
        vm((nx, ny, nz, 16, LANES), BF16),
        vm((nz, 16, LANES), BF16),
        vm((RANK, d), F32),
        vm((tn, RANK, 2 * LANES), F32),
        vm((2 * tn, RANK, 2 * LANES), F32),
        vm((nz, RANK, LANES), F32),
        vm((RANK, LANES), F32),
        pltpu.SemaphoreType.DMA((7,)),
        pltpu.SemaphoreType.DMA((CHANNELS,)),
        pltpu.SemaphoreType.DMA((CHANNELS,)),
        pltpu.SemaphoreType.REGULAR((4,)),
    ]
    anywhere = pl.BlockSpec(memory_space=pl.ANY)
    return pl.pallas_call(
        functools.partial(kernel, nx, ny, nz),
        out_shape=(
            jax.ShapeDtypeStruct((RANK, d), F32),
            jax.ShapeDtypeStruct((RANK, width), F32),
        ),
        in_specs=[anywhere] * 4,
        out_specs=(anywhere, pl.BlockSpec(memory_space=pltpu.VMEM)),
        scratch_shapes=scratch,
        compiler_params=pltpu.CompilerParams(
            collective_id=0, has_side_effects=True, vmem_limit_bytes=54600 * 1024
        ),
    )(start_factor, grad_query, activations, feedback)


def solution(mesh):
    side = 4 if mesh.shape["tensor"] == 16 else 2
    in_specs = (P(("dp", "tensor"), None), P("dp", "tensor"), P("dp", "tensor"), P(None, "tensor"))
    out_specs = (P("tensor", None), P(None, "tensor"))
    return jax.shard_map(
        functools.partial(body, side, mesh.shape["tensor"] // side),
        mesh=mesh, in_specs=in_specs, out_specs=out_specs, check_vma=False,
    )
```

```python
import functools
import itertools

import jax
import jax.numpy as jnp
from jax import lax
from jax.experimental import pallas as pl
from jax.experimental.pallas import tpu as pltpu
from jax.sharding import PartitionSpec as P

EPSILON = 1e-06
MESH = pl.DeviceIdType.MESH
F32, BF16 = jnp.float32, jnp.bfloat16
RANK = 8
LANES = 128
NT = (((1,), (1,)), ((), ()))
NN = (((1,), (0,)), ((), ()))
CHANNELS = 56


def dot(a, b, dims):
    return lax.dot_general(a, b, dims, preferred_element_type=F32)


def pair(value):
    top = value.astype(BF16).astype(F32)
    return jnp.concatenate([top, value - top], axis=0).astype(BF16)


def unpair(value):
    return value[:RANK] + value[RANK:]


def wait_bytes(ref, sem):
    pltpu.make_async_copy(ref, ref, sem).wait()


def hops(k, n):
    return min(k, n - k)


def kernel(
    nx, ny, nz,
    s_hbm, g_hbm, a_hbm, f_hbm,
    basis_hbm, coeffs_ref,
    s_v, g_v, a_v, f_v, gh_v, fh_v,
    psend, precv,
    first, first_in, second, second_in,
    lf, lfr, zs, zr,
    ball, other_half, basis_v,
    qs, qr, cr, cfin,
    local, send, recv, ready,
):
    tn = nx * ny
    half = a_v.shape[1]
    slots = max(nz // 8, 1)
    groups = nz // (2 * slots)
    dp, t = lax.axis_index("dp"), lax.axis_index("tensor")
    z, c = dp // 2, lax.rem(dp, 2)
    o = 1 - c
    x, y = t // ny, lax.rem(t, ny)
    partner = (2 * z + o, t)
    xs = [x] + [lax.rem(x + k, nx) for k in range(1, nx)]
    ys = [y] + [lax.rem(y + k, ny) for k in range(1, ny)]
    around = [z] + [lax.rem(z + k, nz) for k in range(1, nz)]

    def block(index, size):
        return pl.ds(pl.multiple_of(index * size, size), size)

    counter = itertools.count()
    sent = []

    def remote(src, dst, channel, device):
        return pltpu.make_async_remote_copy(
            src_ref=src, dst_ref=dst, send_sem=send.at[channel], recv_sem=recv.at[channel],
            device_id=device, device_id_type=MESH,
        )

    def arrived(ref, channel):
        wait_bytes(ref, recv.at[channel])
        sent.append((ref, channel))

    def along_z(k):
        return (2 * around[k] + c, t)

    def along_x(k):
        return (dp, xs[k] * ny + y)

    def along_y(k):
        return (dp, x * ny + ys[k])

    plane = []
    for dx, dy, dc in itertools.product(range(nx), range(ny), range(2)):
        if dx + dy + dc:
            group = xs[dx] * ny + ys[dy]
            plane.append((hops(dx, nx) + hops(dy, ny), group, (2 * z + o if dc else dp, group), not dc))
    plane.sort(key=lambda entry: -entry[0])
    by_distance = sorted(range(1, nz), key=lambda k: -hops(k, nz))

    load_s = pltpu.make_async_copy(s_hbm, s_v, local.at[0])
    load_g = pltpu.make_async_copy(g_hbm, g_v, local.at[1])
    load_a = pltpu.make_async_copy(a_hbm.at[:, block(c, half)], a_v.at[block(c, LANES), :], local.at[2])
    load_f = pltpu.make_async_copy(f_hbm, f_v, local.at[3])
    load_gh = pltpu.make_async_copy(g_hbm.at[:, block(c, LANES)], gh_v.at[c], local.at[4])
    load_fh = pltpu.make_async_copy(f_hbm.at[:, block(c, LANES)], fh_v.at[c], local.at[5])
    barrier = pltpu.get_barrier_semaphore()
    beside = sorted({1, nz - 1})
    for _, _, device, _ in plane:
        pl.semaphore_signal(barrier, inc=1, device_id=device, device_id_type=MESH)
    for k in beside:
        pl.semaphore_signal(barrier, inc=1, device_id=along_z(k), device_id_type=MESH)
    for load in (load_s, load_g, load_a, load_f, load_gh, load_fh):
        load.start()

    reach = [2 ** k for k in range(8) if 2 ** k < nz // 2]

    def tell(step):
        for k in (reach[step], nz - reach[step]):
            pl.semaphore_signal(ready.at[step], inc=1, device_id=along_z(k), device_id_type=MESH)

    load_s.wait()
    s2 = pair(s_v[...])
    load_g.wait()
    p2 = pair(unpair(dot(s2, g_v[...], NT)))
    for k in range(tn):
        psend[k] = p2[:, k * LANES:(k + 1) * LANES]

    pl.semaphore_wait(barrier, len(plane) + len(beside))

    p_channel = next(counter)
    for _, group, device, _ in plane:
        remote(psend.at[group], precv.at[block(c * tn + t, 16), :], p_channel, device).start()
    share_a = remote(a_hbm.at[:, block(o, half)], a_v.at[block(c, LANES), :], next(counter), partner)
    share_a.start()
    tell(0)
    precv[block(c * tn + t, 16), :] = psend[t]

    load_a.wait()
    share_a.wait()
    arrived(precv.at[pl.ds(0, (2 * tn - 1) * 16), :], p_channel)

    def features(k):
        return a_v[:, block(around[k], LANES)]

    def start(r):
        return r[0] * slots if r[1] == 0 else nz - (r[0] + 1) * slots

    def region(r):
        return range(start(r), start(r) + slots)

    def order(r):
        on_x, on_y = (x, nx, xs, along_x), (y, ny, ys, along_y)
        return (on_y, on_x) if r[1] else (on_x, on_y)

    def part_of(r):
        return pl.ds(start(r), slots)

    wide = first.shape[-1] // LANES

    def wide_region(r):
        begin = r[0] * wide if r[1] == 0 else nz - (r[0] + 1) * wide
        return range(begin, begin + wide)

    def index(r):
        return 2 * r[0] + r[1]

    nearest = [(i, side) for i in range(groups) for side in range(2)]
    farthest = [(i, side) for i in reversed(range(nz // (2 * wide))) for side in range(2)]

    lhs = jnp.concatenate([precv[:tn * 16, :], precv[tn * 16:, :]], axis=1)
    first_channel, second_channel = {}, {}
    for r in farthest:
        (here, count, _, device), _ = order(r)
        part = dot(lhs, jnp.concatenate([features(k) for k in wide_region(r)], axis=1), NN)
        for gx in range(nx):
            for gy in range(ny):
                g = gx * ny + gy
                i, j = (gy, gx) if r[1] else (gx, gy)
                first[index(r), i, j] = unpair(part[g * 16:(g + 1) * 16])
        first_channel[r] = next(counter)
        others = order(r)[0][2]
        for k in range(1, count):
            remote(first.at[index(r), others[k]], first_in.at[index(r), here], first_channel[r], device(k)).start()
    if len(reach) > 1:
        pl.semaphore_wait(ready.at[0], 2)
        tell(1)

    load_f.wait()
    for h in range(2):
        for k in range(nz):
            at = (h * nz + k) * LANES
            lf[h, k] = unpair(dot(s2, f_v[at:at + LANES, :], NT))
    share_l = remote(lf.at[o], lfr, next(counter), partner)
    share_l.start()

    def pass_on(r):
        (here, count, others, _), (place, size, beyond, device) = order(r)
        arrived(first_in.at[index(r), pl.ds(0, count - 1)], first_channel[r])
        total = first[index(r), here]
        for k in range(1, count):
            total = total + first_in[index(r), others[k]]
        second[index(r)] = total
        second_channel[r] = next(counter)
        for k in range(1, size):
            remote(second.at[index(r), beyond[k]], second_in.at[index(r), place], second_channel[r], device(k)).start()

    z_channel = next(counter)

    def pass_along_z(r):
        _, (place, size, beyond, _) = order(r)
        arrived(second_in.at[index(r), pl.ds(0, size - 1)], second_channel[r])
        total = second[index(r), place]
        for k in range(1, size):
            total = total + second_in[index(r), beyond[k]]
        for i, k in enumerate(wide_region(r)):
            zs[k] = total[:, i * LANES:(i + 1) * LANES] + (lf[c, around[k]] + lfr[around[k]])
        for k in sorted(wide_region(r), key=lambda k: -hops(k, nz)):
            if k:
                remote(zs.at[k], zr.at[k], z_channel, along_z(k)).start()

    ahead = len(farthest) - 2
    for r in farthest[:ahead]:
        pass_on(r)
    if len(reach) > 2:
        pl.semaphore_wait(ready.at[1], 2)
        tell(2)
    share_l.wait()
    for step in range(max(len(reach) - 1, 0), len(reach)):
        pl.semaphore_wait(ready.at[step], 2)
    for r, late in itertools.zip_longest(farthest, farthest[ahead:]):
        pass_along_z(r)
        if late:
            pass_on(late)
    share_g = remote(g_hbm.at[:, block(o, LANES)], gh_v.at[c], next(counter), partner)
    share_g.start()
    share_f = remote(f_hbm.at[:, block(o, LANES)], fh_v.at[c], next(counter), partner)
    share_f.start()
    arrived(zr.at[pl.ds(0, nz - 1)], z_channel)
    total = zs[0]
    for k in range(1, nz):
        total = total + zr[k]

    ball[x, y, 0] = pair(total)
    gather = {r: next(counter) for r in nearest}
    for k in by_distance:
        r = next(r for r in nearest if k in region(r))
        remote(ball.at[x, y, 0], ball.at[x, y, k], gather[r], along_z(nz - k)).start()

    def spread_own(r):
        own = part_of(r)
        if r == nearest[0]:
            if slots > 1:
                arrived(ball.at[x, y, pl.ds(0, slots - 1)], gather[r])
        else:
            arrived(ball.at[x, y, own], gather[r])
        first_channel[r] = next(counter)
        (_, count, _, device), _ = order(r)
        for k in range(1, count):
            remote(ball.at[x, y, own], ball.at[x, y, own], first_channel[r], device(k)).start()

    def span(members, side):
        begin = start((members[-1] if side else members[0], side))
        return range(begin, begin + len(members) * slots)

    def spread_lines(members, side):
        (_, count, _, _), (_, size, _, device) = order((0, side))
        for i in members:
            arrived(ball.at[x, pl.ds(0, count - 1), part_of((i, side))], first_channel[i, side])
        own = pl.ds(span(members, side)[0], len(members) * slots)
        second_channel[members[0], side] = next(counter)
        line = ball.at[x, :, own] if side else ball.at[:, y, own]
        for k in range(1, size):
            remote(line, line, second_channel[members[0], side], device(k)).start()

    def columns(slots_of):
        return jnp.concatenate([features(k) for k in slots_of], axis=1)

    def lines(slots_of):
        return jnp.concatenate([ball[:, :, k].reshape(tn * 16, LANES) for k in slots_of], axis=1)

    def product(members, side):
        chunks = span(members, side)
        own = pl.ds(chunks[0], len(chunks))
        size = order((0, side))[1][1]
        rest = ball.at[pl.ds(0, size - 1), :, own] if side else ball.at[:, pl.ds(0, size - 1), own]
        arrived(rest, second_channel[members[0], side])
        return dot(lines(chunks), columns(chunks), NT)

    last = groups - 1
    opposite = range(start((last, 0)), start((last, 1)) + slots)
    for step in range(last):
        spread_own((step, 0))
        spread_own((step, 1))
    for side in range(2):
        arrived(ball.at[x, y, part_of((last, side))], gather[last, side])
    straight = next(counter)
    far = pl.ds(opposite[0], len(opposite))
    for _, _, device, same in plane:
        if same:
            remote(ball.at[x, y, far], ball.at[x, y, far], straight, device).start()
    share_half = remote(ball.at[x, y], other_half, next(counter), partner)
    share_half.start()
    joined = [list(range(last - 1)), [last - 1]] if last > 1 else [[0]]
    for members in joined:
        for side in range(2):
            spread_lines(members, side)

    share_half.wait()
    pairs = []
    for h in range(2):
        for k in range(nz):
            slot = lax.rem(k - z + nz, nz)
            pairs.append(jnp.where(c == h, ball[x, y, slot].astype(F32), other_half[slot].astype(F32)))
    v = [unpair(u) for u in pairs]
    row = lax.broadcasted_iota(jnp.int32, (RANK, 1), 0)
    ops = (lax.broadcasted_iota(jnp.int32, (RANK, LANES), 0) == lax.broadcasted_iota(jnp.int32, (RANK, LANES), 1)).astype(F32)
    scale = jnp.zeros((RANK, 1), F32)
    for i in range(RANK):
        own = [jnp.broadcast_to(u[i:i + 1, :], u.shape) for u in v]
        prods = [a * b for a, b in zip(own, v)]
        while len(prods) > 1:
            prods = [a + b for a, b in zip(prods[::2], prods[1::2])]
        dots = jnp.sum(prods[0], axis=1, keepdims=True)
        square = dots[i:i + 1, :] + EPSILON
        scale = jnp.where(row == i, 1.0 / jnp.sqrt(square), scale)
        factor = jnp.where(row > i, dots / square, 0.0)
        v = [u - factor * a for u, a in zip(v, own)]
        ops = ops - factor * jnp.broadcast_to(ops[i:i + 1, :], ops.shape)
    ops = ops * scale
    for k, u in enumerate(v):
        basis_v[:, k * LANES:(k + 1) * LANES] = u * scale
    store_basis = pltpu.make_async_copy(basis_v, basis_hbm, local.at[6])
    store_basis.start()

    load_fh.wait()
    share_f.wait()
    left = jnp.concatenate([u.astype(BF16) for u in pairs], axis=1)
    right = dot(left, fh_v[0], NN) + dot(left, fh_v[1], NN)

    q2 = sum(product(members, side) for members in joined for side in range(2))
    arrived(ball.at[pl.ds(0, len(opposite)), 0, pl.ds(0, tn - 1)], straight)
    q2 = q2 + dot(lines(opposite), columns(opposite), NT)
    for g in range(tn):
        qs[g] = unpair(q2[g * 16:(g + 1) * 16])
    q_channel = next(counter)
    for _, group, device, _ in plane:
        remote(qs.at[group], qr.at[c * tn + t], q_channel, device).start()
    qr[c * tn + t] = qs[t]

    load_gh.wait()
    share_g.wait()
    arrived(qr.at[pl.ds(0, 2 * tn - 1)], q_channel)
    parts = [pair(qr[k] + qr[tn + k]) for k in range(tn)]
    for h in range(2):
        q = jnp.concatenate([u[:, h * LANES:(h + 1) * LANES] for u in parts], axis=1)
        right = right + dot(q, gh_v[h], NN)
    right = unpair(right)
    cr[z] = sum(ops[:, i:i + 1] * right[i:i + 1, :] for i in range(RANK))

    c_channel = next(counter)
    for k in by_distance:
        remote(cr.at[z], cr.at[z], c_channel, along_z(k)).start()
    store_basis.wait()
    for ref, channel in sent:
        wait_bytes(ref, send.at[channel])
    wait_bytes(cr.at[pl.ds(0, nz - 1)], recv.at[c_channel])
    total = cr[0]
    for k in range(1, nz):
        total = total + cr[k]
    total = total * (1.0 / (2 * nz))
    cfin[...] = total
    coeffs_ref[:, block(c, LANES)] = total
    share_c = remote(cfin, coeffs_ref.at[:, block(c, LANES)], next(counter), partner)
    share_c.start()

    wait_bytes(cr.at[pl.ds(0, nz - 1)], send.at[c_channel])
    share_c.wait()


def body(nx, ny, activations, grad_query, feedback, start_factor):
    tn = nx * ny
    nz = lax.axis_size("dp") // 2
    d = activations.shape[1]
    half = d // 2
    wide = max(nz // 4, 1)
    regions, part = nz // wide, wide * LANES
    tok, width = grad_query.shape
    vm = pltpu.VMEM
    side = max(nx, ny)
    scratch = [
        vm((RANK, width), F32),
        vm((tok, width), BF16),
        vm((2 * LANES, half), BF16),
        vm((d, width), BF16),
        vm((2, tok, LANES), BF16),
        vm((2, d, LANES), BF16),
        vm((tn, 16, LANES), BF16),
        vm((2 * tn * 16, LANES), BF16),
        vm((regions, side, side, RANK, part), F32),
        vm((regions, side, side, RANK, part), F32),
        vm((regions, side, RANK, part), F32),
        vm((regions, side, RANK, part), F32),
        vm((2, nz, RANK, LANES), F32),
        vm((nz, RANK, LANES), F32),
        vm((nz, RANK, LANES), F32),
        vm((nz, RANK, LANES), F32),
        vm((nx, ny, nz, 16, LANES), BF16),
        vm((nz, 16, LANES), BF16),
        vm((RANK, d), F32),
        vm((tn, RANK, 2 * LANES), F32),
        vm((2 * tn, RANK, 2 * LANES), F32),
        vm((nz, RANK, LANES), F32),
        vm((RANK, LANES), F32),
        pltpu.SemaphoreType.DMA((7,)),
        pltpu.SemaphoreType.DMA((CHANNELS,)),
        pltpu.SemaphoreType.DMA((CHANNELS,)),
        pltpu.SemaphoreType.REGULAR((4,)),
    ]
    anywhere = pl.BlockSpec(memory_space=pl.ANY)
    return pl.pallas_call(
        functools.partial(kernel, nx, ny, nz),
        out_shape=(
            jax.ShapeDtypeStruct((RANK, d), F32),
            jax.ShapeDtypeStruct((RANK, width), F32),
        ),
        in_specs=[anywhere] * 4,
        out_specs=(anywhere, pl.BlockSpec(memory_space=pltpu.VMEM)),
        scratch_shapes=scratch,
        compiler_params=pltpu.CompilerParams(
            collective_id=0, has_side_effects=True, vmem_limit_bytes=54600 * 1024
        ),
    )(start_factor, grad_query, activations, feedback)


def solution(mesh):
    side = 4 if mesh.shape["tensor"] == 16 else 2
    in_specs = (P(("dp", "tensor"), None), P("dp", "tensor"), P("dp", "tensor"), P(None, "tensor"))
    out_specs = (P("tensor", None), P(None, "tensor"))
    return jax.shard_map(
        functools.partial(body, side, mesh.shape["tensor"] // side),
        mesh=mesh, in_specs=in_specs, out_specs=out_specs, check_vma=False,
    )
```
